256 devices in a mesh: shot: 2 (over z_lo), gx: 32 (over x, z_hi, core), gy: 4 (over y).
Axes of the slice: x: 4, y: 4, z: 8 (z_hi: 4, z_lo: 2; z = z_hi * 2 + z_lo), core: 2. Of those that a mesh axis runs over, the one named last changes fastest.
Arguments:
- velocity: float32 [256, 32, 256], P('gx', 'gy', 'shot'), may hold values from 0.2 to 0.42
- density: float32 [256, 32, 256], P('gx', 'gy', 'shot'), may hold values from 1 to 4
- stored_fields: float32 [1024, 2, 16, 256], P('gx', None, ('shot', 'gy')), may hold values from -6 to 6
- holders: int32 [32, 32], P('gx'), may hold values from 0 to 31, each once within a row
- adjoint_init: float32 [2, 2, 256, 32, 256], P('shot', None, 'gx', 'gy'), may hold values from -6 to 6
- traces: float32 [2, 4, 256, 32], P('shot', None, 'gx', 'gy'), may hold values from -24 to 24
- aperture: int32 [2, 2], replicated, may hold values from 0 to 32, as said below
Outputs:
- image: float32 [256, 32, 256], P('gx', 'gy', 'shot')
- forward_end: float32 [2, 2, 256, 32, 256], P('shot', None, 'gx', 'gy')
- adjoint_end: float32 [2, 2, 256, 32, 256], P('shot', None, 'gx', 'gy')
The draws below stay inside these ranges and needn't reach their ends.
Inputs may be any that keep to these rules, and one draw needn't show every extreme that they name: Each row of holders is a permutation of 0 to 31. aperture[s, 0] < aperture[s, 1] for every shot.
All inputs are finite; a program needn't handle non-finite values.
Results may differ from the reference program's by a relative error of at most 0.00002.
Values sent between devices are 32-bit elements; how exact they have to be, the bound alone decides.
A program may use at most 192 MiB of HBM per device.

```python
import math
import jax
import jax.numpy as jnp

CX = 8
CY = 8
NZ = 256
STEPS = 4
REC_Z = 8
SHOTS = 2
NX = 256
NY = 32
PR = 2
N_GX = 32
N_GY = 4


def draw_aperture(key, part):
    key = jax.random.fold_in(key, 7)
    first_key, second_key = jax.random.split(key)
    starts = jax.random.randint(first_key, (SHOTS,), 0, N_GX // 2 + 1)
    ends = jax.random.randint(second_key, (SHOTS,), N_GX // 2 + 1, N_GX + 1)
    starts = starts.at[0].set(0)
    ends = ends.at[SHOTS - 1].set(N_GX)
    return jnp.stack([starts, ends], axis=1).astype(jnp.int32)


def levels(rng, dims, cuts, low, high):
    def one(axis_at, parts):
        steps = jax.random.uniform(jax.random.fold_in(jax.random.fold_in(rng, 6), axis_at), (parts,), jnp.float32, low / len(cuts), high / len(cuts))
        return jnp.repeat(jnp.exp(steps), dims[axis_at] // parts).reshape((-1,) + (1,) * (len(dims) - axis_at - 1))

    factor_of = one(*cuts[0])
    for cut in cuts[1:]:
        factor_of = factor_of * one(*cut)
    return factor_of


def gaussian(rng, shape, width, bound, shards=(), kind=jnp.bfloat16):
    entries = width * jax.random.normal(rng, shape, jnp.float32)
    if shards:
        entries = entries * levels(rng, shape, shards, -0.22, 0.18)
    return jnp.clip(entries, -bound, bound).astype(kind)


def setup_inputs(seed: int = 0) -> dict:
    seeds = jax.random.split(jax.random.key(seed), 8)
    return {
        "velocity": jnp.clip(0.2 + 0.21999998 * jax.random.uniform(seeds[0], (NX, NY, NZ), jnp.float32) ** levels(seeds[0], (NX, NY, NZ), ((0, 32), (1, 4), (2, 2)), -0.2, 0.2), 0.2, 0.42),
        "density": jnp.clip(jnp.exp(math.log(4.0) - 1.3862944 * jax.random.uniform(seeds[1], (NX, NY, NZ), jnp.float32) ** levels(seeds[1], (NX, NY, NZ), ((0, 32), (1, 4), (2, 2)), -0.2, 0.2)), 1.0, 4.0),
        "stored_fields": gaussian(seeds[2], (N_GX * N_GX, 2, SHOTS * N_GY * PR, NZ), 1.0, 6.0, ((0, 32), (2, 8)), jnp.float32),
        "holders": jax.vmap(lambda own: jax.random.permutation(own, N_GX))(jax.random.split(seeds[3], N_GX)).reshape((N_GX, N_GX)).astype(jnp.int32),
        "adjoint_init": gaussian(seeds[4], (SHOTS, 2, NX, NY, NZ), 1.0, 6.0, ((0, 2), (2, 32), (3, 4)), jnp.float32),
        "traces": gaussian(seeds[5], (SHOTS, STEPS, NX, NY), 4.0, 24.0, ((0, 2), (2, 32), (3, 4)), jnp.float32),
        "aperture": draw_aperture(jax.random.fold_in(seeds[7], 71), 0),
    }


LAPLACE_TAPS = (-205.0 / 72.0, 8.0 / 5.0, -1.0 / 5.0, 8.0 / 315.0, -1.0 / 560.0)
SLOPE_TAPS = (4.0 / 5.0, -1.0 / 5.0, 4.0 / 105.0, -1.0 / 280.0)


def window(extended, offsets):
    lengths = [extended.shape[extended.ndim - 3 + dimension] - 8 for dimension in range(3)]
    starts = [4 + offsets[dimension] for dimension in range(3)]
    return extended[..., starts[0]:starts[0] + lengths[0], starts[1]:starts[1] + lengths[1], starts[2]:starts[2] + lengths[2]]


def moved(spatial, amount):
    offsets = [0, 0, 0]
    offsets[spatial] = amount
    return tuple(offsets)


def laplace(extended):
    summed = (3.0 * LAPLACE_TAPS[0]) * window(extended, (0, 0, 0))
    for radius in range(1, 5):
        paired = window(extended, moved(0, radius)) + window(extended, moved(0, -radius))
        for spatial in (1, 2):
            paired = paired + window(extended, moved(spatial, radius)) + window(extended, moved(spatial, -radius))
        summed = summed + LAPLACE_TAPS[radius] * paired
    return summed


def slope(extended, spatial):
    summed = SLOPE_TAPS[0] * (window(extended, moved(spatial, 1)) - window(extended, moved(spatial, -1)))
    for radius in range(2, 5):
        summed = summed + SLOPE_TAPS[radius - 1] * (window(extended, moved(spatial, radius)) - window(extended, moved(spatial, -radius)))
    return summed


def advance(extended, previous, speed_sq, log_grads):
    advection = log_grads[0] * slope(extended, 0) + log_grads[1] * slope(extended, 1) + log_grads[2] * slope(extended, 2)
    return 2.0 * window(extended, (0, 0, 0)) - previous + speed_sq * (laplace(extended) - advection)


def pad_space(field):
    widths = [(0, 0)] * (field.ndim - 3) + [(4, 4), (4, 4), (4, 4)]
    return jnp.pad(field, widths)


def reference(velocity, density, stored_fields, holders, adjoint_init, traces, aperture):
    speed_sq = velocity * velocity
    log_density = jnp.log(density)
    padded_log = pad_space(log_density)
    log_grads = [slope(padded_log, spatial) for spatial in range(3)]
    stacked = stored_fields.reshape(N_GX, N_GX, 2, SHOTS, N_GY, PR, NZ)
    holder_of = jnp.argsort(holders, axis=1).astype(jnp.int32)
    pieces = stacked[holder_of, jnp.arange(N_GX, dtype=jnp.int32)[:, None]]
    pieces = jnp.transpose(pieces, (3, 2, 0, 4, 1, 5, 6)).reshape(SHOTS, 2, N_GX, N_GY, CX, CY, NZ)
    forward = jnp.transpose(pieces, (0, 1, 2, 4, 3, 5, 6)).reshape(SHOTS, 2, NX, NY, NZ)
    current = jnp.stack([forward[:, 0], adjoint_init[:, 0]], axis=1)
    previous = jnp.stack([forward[:, 1], adjoint_init[:, 1]], axis=1)
    forwards = {}
    backwards = {STEPS: adjoint_init[:, 0]}
    for number in range(1, STEPS + 1):
        advanced = advance(pad_space(current), previous, speed_sq, log_grads)
        injected = speed_sq[:, :, REC_Z][None] * traces[:, STEPS - number]
        advanced = advanced.at[:, 1, :, :, REC_Z].add(injected)
        previous, current = current, advanced
        forwards[number] = current[:, 0]
        backwards[STEPS - number] = current[:, 1]
    correlation = forwards[1] * backwards[1]
    for number in range(2, STEPS + 1):
        correlation = correlation + forwards[number] * backwards[number]
    block_of = jnp.arange(NX, dtype=jnp.int32) // CX
    masks = ((block_of[None, :] >= aperture[:, 0:1]) & (block_of[None, :] < aperture[:, 1:2])).astype(jnp.float32)
    image = jnp.sum(masks[:, :, None, None] * correlation, axis=0)
    forward_end = jnp.stack([forwards[STEPS], forwards[STEPS - 1]], axis=1)
    adjoint_end = jnp.stack([backwards[0], backwards[1]], axis=1)
    return image, forward_end, adjoint_end
```

```python
import functools

import jax
import jax.numpy as jnp
from jax import lax
from jax.experimental import pallas as pl
from jax.experimental.pallas import tpu as pltpu
from jax.sharding import PartitionSpec as P

REC_Z = 8
STEPS = 4
LAPLACE_TAPS = (-205.0 / 72.0, 8.0 / 5.0, -1.0 / 5.0, 8.0 / 315.0, -1.0 / 560.0)
SLOPE_TAPS = (4.0 / 5.0, -1.0 / 5.0, 4.0 / 105.0, -1.0 / 280.0)


def y_plus(centre, halo, row, k):
    return pltpu.roll(jnp.where(row < k, halo, centre), 8 - k, 1)


def y_minus(centre, halo, row, k):
    return pltpu.roll(jnp.where(row >= 8 - k, halo, centre), k, 1)


def z_plus(lower, upper, lane, k):
    low, up = pltpu.roll(lower, 128 - k, 2), pltpu.roll(upper, 128 - k, 2)
    return jnp.where(lane < 128 - k, low, up), up


def z_minus(lower, upper, lane, k):
    low, up = pltpu.roll(lower, k, 2), pltpu.roll(upper, k, 2)
    return low, jnp.where(lane >= k, up, low)


def kernel(
    n_x,
    n_y,
    velocity,
    density,
    stored,
    holders,
    adjoint,
    traces,
    aperture,
    image_out,
    forward_out,
    adjoint_out,
    field,
    halo,
    before,
    last,
    coef,
    dens,
    dens_y,
    speed,
    pieces,
    holders_v,
    traces_v,
    aperture_v,
    inject,
    share,
    partner_share,
    image_v,
    small_sem,
    local_sem,
    own_sem,
    piece_sem,
    model_sem,
    send_sem,
    halo_send,
    halo_recv,
    image_sem,
    out_sem,
):
    s, b, j = lax.axis_index("shot"), lax.axis_index("gx"), lax.axis_index("gy")
    other = 1 - s
    right, left = lax.rem(b + 1, n_x), lax.rem(b + n_x - 1, n_x)
    up, down = lax.rem(j + 1, n_y), lax.rem(j + n_y - 1, n_y)

    smalls = [
        pltpu.make_async_copy(holders, holders_v, small_sem.at[0]),
        pltpu.make_async_copy(traces.at[0], traces_v, small_sem.at[1]),
        pltpu.make_async_copy(aperture, aperture_v, small_sem.at[2]),
    ]
    owns = [
        pltpu.make_async_copy(adjoint.at[0, 0], field.at[1, 0, pl.ds(4, 8)], own_sem.at[0]),
        pltpu.make_async_copy(adjoint.at[0, 1], before.at[1], own_sem.at[1]),
    ]
    own_model = [
        pltpu.make_async_copy(density, dens.at[s, pl.ds(4, 8)], local_sem.at[0]),
        pltpu.make_async_copy(velocity, speed.at[s], local_sem.at[1]),
        pltpu.make_async_copy(stored.at[b], pieces.at[b], local_sem.at[2]),
    ]
    for copy in smalls + owns + own_model:
        copy.start()

    barrier = pltpu.get_barrier_semaphore()

    def greet(step, carry):
        pl.semaphore_signal(barrier, inc=1, device_id={"gx": lax.rem(b + step, n_x)})
        return carry

    lax.fori_loop(1, n_x, greet, 0)
    near = [
        {"shot": other},
        {"shot": other, "gx": right},
        {"shot": other, "gx": left},
        {"gy": up},
        {"gy": down},
        {"shot": other, "gy": up},
        {"shot": other, "gy": down},
    ]
    for target in near:
        pl.semaphore_signal(barrier, inc=1, device_id=target)
    pl.semaphore_wait(barrier, n_x - 1 + len(near))

    def send_piece(step, carry):
        target = lax.rem(b + step, n_x)
        pltpu.make_async_remote_copy(
            stored.at[target], pieces.at[b], send_sem.at[0], piece_sem, device_id={"gx": target}
        ).start()
        return carry

    lax.fori_loop(1, n_x, send_piece, 0)

    def halo_sends(which, level, source):
        edges = [
            (source(pl.ds(4, 4), None), field.at[which, level, pl.ds(0, 4)], {"gx": right}),
            (source(pl.ds(0, 4), None), field.at[which, level, pl.ds(12, 4)], {"gx": left}),
            (source(pl.ds(0, 8), pl.ds(0, 4)), halo.at[which, level, :, pl.ds(0, 4)], {"gy": down}),
            (source(pl.ds(0, 8), pl.ds(4, 4)), halo.at[which, level, :, pl.ds(4, 4)], {"gy": up}),
        ]
        copies = []
        for side, (src, dst, target) in enumerate(edges):
            copies.append(
                pltpu.make_async_remote_copy(
                    src,
                    dst,
                    halo_send.at[which, level, side],
                    halo_recv.at[which, level, side],
                    device_id=target,
                )
            )
        for copy in copies:
            copy.start()
        return copies

    def from_argument(planes, rows):
        return adjoint.at[0, 0, planes] if rows is None else adjoint.at[0, 0, planes, rows]

    def from_field(which, level):
        def source(planes, rows):
            planes = pl.ds(planes.start + 4, planes.size)
            if rows is None:
                return field.at[which, level, planes]
            return field.at[which, level, planes, rows]

        return source

    sends = {(1, 0): halo_sends(1, 0, from_argument)}

    model = [
        (velocity, speed.at[s], {"shot": other}),
        (density, dens.at[s, pl.ds(4, 8)], {"shot": other}),
    ]
    for place in (s, other):
        model += [
            (density.at[pl.ds(4, 4)], dens.at[s, pl.ds(0, 4)], {"shot": place, "gx": right}),
            (density.at[pl.ds(0, 4)], dens.at[s, pl.ds(12, 4)], {"shot": place, "gx": left}),
            (density.at[:, pl.ds(0, 4)], dens_y.at[s, :, pl.ds(0, 4)], {"shot": place, "gy": down}),
            (density.at[:, pl.ds(4, 4)], dens_y.at[s, :, pl.ds(4, 4)], {"shot": place, "gy": up}),
        ]
    model_copies = []
    for at, (src, dst, target) in enumerate(model):
        copy = pltpu.make_async_remote_copy(
            src, dst, send_sem.at[1 + at], model_sem.at[at], device_id=target
        )
        copy.start()
        model_copies.append(copy)

    row = lax.broadcasted_iota(jnp.int32, (8, 8, 128), 1)
    lane = lax.broadcasted_iota(jnp.int32, (8, 8, 128), 2)
    low, high = pl.ds(0, 128), pl.ds(128, 128)

    for copy in smalls:
        copy.wait()
    column = lax.broadcasted_iota(jnp.int32, (64, n_x), 0)
    place = column // 2
    parity = column - 2 * place
    hit = holders_v[...] == place
    picks = [jnp.where(hit & (parity == r), 1.0, 0.0).astype(jnp.float32) for r in range(2)]

    bounds = aperture_v[...]
    bounds = jnp.where(s == 0, bounds[0:1], bounds[1:2])
    active = jnp.where((b >= bounds[:, 0:1]) & (b < bounds[:, 1:2]), 1.0, 0.0).astype(jnp.float32)
    active = active.reshape(1, 1, 1)

    for copy in own_model[:2]:
        copy.wait()
    for copy in model_copies:
        copy.wait_recv()

    first_x, last_x = b == 0, b == n_x - 1
    first_y, last_y = j == 0, j == n_y - 1
    keep_left = jnp.where(first_x, 0.0, 1.0).astype(jnp.float32)
    keep_right = jnp.where(last_x, 0.0, 1.0).astype(jnp.float32)
    keep_down = jnp.where(first_y, 0.0, 1.0).astype(jnp.float32)
    keep_up = jnp.where(last_y, 0.0, 1.0).astype(jnp.float32)
    logs, logs_y = [], []
    for half in range(2):
        wide = jnp.log(dens[half])
        logs.append(
            jnp.concatenate([wide[:4] * keep_left, wide[4:12], wide[12:] * keep_right], axis=0)
        )
        logs_y.append(jnp.log(dens_y[half]) * jnp.where(row < 4, keep_up, keep_down))
    inner = [logs[half][4:12] for half in range(2)]
    grad_x, grad_y, grad_z = [0.0, 0.0], [0.0, 0.0], [0.0, 0.0]
    for k in range(1, 5):
        tap = SLOPE_TAPS[k - 1]
        ahead = z_plus(inner[0], inner[1], lane, k)
        behind = z_minus(inner[0], inner[1], lane, k)
        ahead = (ahead[0], jnp.where(lane < 128 - k, ahead[1], 0.0))
        behind = (jnp.where(lane >= k, behind[0], 0.0), behind[1])
        for half in range(2):
            wide = logs[half]
            grad_x[half] += tap * (wide[4 + k : 12 + k] - wide[4 - k : 12 - k])
            grad_y[half] += tap * (
                y_plus(inner[half], logs_y[half], row, k)
                - y_minus(inner[half], logs_y[half], row, k)
            )
            grad_z[half] += tap * (ahead[half] - behind[half])

    for half, lanes in enumerate((low, high)):
        root = speed[half]
        sq = root * root
        coef[0, :, :, lanes] = 2.0 + (3.0 * LAPLACE_TAPS[0]) * sq
        for k in range(1, 5):
            even = LAPLACE_TAPS[k] * sq
            at = 1 + 6 * (k - 1)
            odd = SLOPE_TAPS[k - 1] * (sq * grad_x[half])
            plus, minus = even - odd, even + odd
            coef[at, : 8 - k, :, lanes] = plus[: 8 - k]
            coef[at, 8 - k :, :, lanes] = plus[8 - k :] * keep_right
            coef[at + 1, :k, :, lanes] = minus[:k] * keep_left
            coef[at + 1, k:, :, lanes] = minus[k:]
            odd = SLOPE_TAPS[k - 1] * (sq * grad_y[half])
            coef[at + 2, :, :, lanes] = (even - odd) * jnp.where(row >= 8 - k, keep_up, 1.0)
            coef[at + 3, :, :, lanes] = (even + odd) * jnp.where(row < k, keep_down, 1.0)
            odd = SLOPE_TAPS[k - 1] * (sq * grad_z[half])
            plus, minus = even - odd, even + odd
            if half == 0:
                minus = jnp.where(lane >= k, minus, 0.0)
            else:
                plus = jnp.where(lane < 128 - k, plus, 0.0)
            coef[at + 4, :, :, lanes] = plus
            coef[at + 5, :, :, lanes] = minus
        if half == 0:
            eye = lax.broadcasted_iota(jnp.int32, (8, 8), 0) == lax.broadcasted_iota(
                jnp.int32, (8, 8), 1
            )
            at_receiver = lax.broadcasted_iota(jnp.int32, (8, 128), 1) == REC_Z
            for number in range(STEPS):
                for x in range(8):
                    line = jnp.where(eye, traces_v[number, pl.ds(x, 1), :], 0.0)
                    line = jnp.sum(line, axis=1, keepdims=True)
                    inject[number, x] = jnp.where(at_receiver, line, 0.0) * sq[x]

    def advance(which, level):
        previous = before.at[which] if level == 0 else field.at[which, level - 1, pl.ds(4, 8)]
        wide = field.at[which, level]
        centre = [wide[4:12, :, lanes] for lanes in (low, high)]
        edge = [halo[which, level, :, :, lanes] for lanes in (low, high)]
        total = [
            coef[0, :, :, lanes] * centre[half] - previous[:, :, lanes]
            for half, lanes in enumerate((low, high))
        ]
        for k in range(1, 5):
            at = 1 + 6 * (k - 1)
            ahead = z_plus(centre[0], centre[1], lane, k)
            behind = z_minus(centre[0], centre[1], lane, k)
            for half, lanes in enumerate((low, high)):
                total[half] = (
                    total[half]
                    + coef[at, :, :, lanes] * wide[4 + k : 12 + k, :, lanes]
                    + coef[at + 1, :, :, lanes] * wide[4 - k : 12 - k, :, lanes]
                    + coef[at + 2, :, :, lanes] * y_plus(centre[half], edge[half], row, k)
                    + coef[at + 3, :, :, lanes] * y_minus(centre[half], edge[half], row, k)
                    + coef[at + 4, :, :, lanes] * ahead[half]
                    + coef[at + 5, :, :, lanes] * behind[half]
                )
        if which == 1:
            total[0] = total[0] + inject[STEPS - 1 - level]
        return total

    def step(which, level):
        for copy in sends[which, level]:
            copy.wait_recv()
        new = advance(which, level)
        if level == STEPS - 1:
            for half, lanes in enumerate((low, high)):
                last[which, :, :, lanes] = new[half]
            return
        for half, lanes in enumerate((low, high)):
            field[which, level + 1, 4:12, :, lanes] = new[half]
        sends[which, level + 1] = halo_sends(which, level + 1, from_field(which, level + 1))

    for copy in owns:
        copy.wait()
    step(1, 0)

    own_model[2].wait()
    pltpu.make_async_copy(pieces.at[pl.ds(0, n_x - 1)], pieces.at[pl.ds(0, n_x - 1)], piece_sem).wait()
    for level in (0, 1):
        found = 0.0
        for r in range(2):
            found += jnp.dot(
                picks[r],
                pieces[:, level, r, :],
                precision=lax.Precision.HIGHEST,
                preferred_element_type=jnp.float32,
            )
        found = found.reshape(8, 8, 256)
        if level == 0:
            field[0, 0, 4:12] = found
            sends[0, 0] = halo_sends(0, 0, from_field(0, 0))
        else:
            before[0] = found

    step(1, 1)
    step(0, 0)
    step(1, 2)
    outs = [
        pltpu.make_async_copy(field.at[1, 3, pl.ds(4, 8)], adjoint_out.at[0, 1], out_sem.at[0])
    ]
    outs[0].start()
    step(0, 1)
    step(1, 3)
    outs.append(pltpu.make_async_copy(last.at[1], adjoint_out.at[0, 0], out_sem.at[1]))
    outs[1].start()
    step(0, 2)
    outs.append(
        pltpu.make_async_copy(field.at[0, 3, pl.ds(4, 8)], forward_out.at[0, 1], out_sem.at[2])
    )
    outs[2].start()
    early = [0.0, 0.0]
    for number in range(1, STEPS):
        for half, lanes in enumerate((low, high)):
            early[half] += (
                field[0, number, 4:12, :, lanes] * field[1, STEPS - number, 4:12, :, lanes]
            )
    step(0, 3)
    outs.append(pltpu.make_async_copy(last.at[0], forward_out.at[0, 0], out_sem.at[3]))
    outs[3].start()
    whole = [
        active * (early[half] + last[0, :, :, lanes] * field[1, 0, 4:12, :, lanes])
        for half, lanes in enumerate((low, high))
    ]
    share[...] = jnp.where(s == 0, whole[1], whole[0])
    to_partner = pltpu.make_async_remote_copy(
        share, partner_share, image_sem.at[0], image_sem.at[1], device_id={"shot": other}
    )
    to_partner.start()
    mine = jnp.where(s == 0, whole[0], whole[1])

    pltpu.make_async_copy(
        stored.at[pl.ds(0, n_x - 1)], stored.at[pl.ds(0, n_x - 1)], send_sem.at[0]
    ).wait()
    for copy in model_copies:
        copy.wait_send()
    for copies in sends.values():
        for copy in copies:
            copy.wait_send()

    to_partner.wait()
    image_v[...] = mine + partner_share[...]
    outs.append(pltpu.make_async_copy(image_v, image_out, out_sem.at[4]))
    outs[4].start()
    for copy in outs:
        copy.wait()


def shards(n_x, n_y, velocity, density, stored, holders, adjoint, traces, aperture):
    f32 = jnp.float32
    anywhere = pl.BlockSpec(memory_space=pl.ANY)
    return pl.pallas_call(
        functools.partial(kernel, n_x, n_y),
        out_shape=(
            jax.ShapeDtypeStruct((8, 8, 128), f32),
            jax.ShapeDtypeStruct((1, 2, 8, 8, 256), f32),
            jax.ShapeDtypeStruct((1, 2, 8, 8, 256), f32),
        ),
        in_specs=[anywhere] * 7,
        out_specs=(anywhere,) * 3,
        scratch_shapes=[
            pltpu.VMEM((2, STEPS, 16, 8, 256), f32),
            pltpu.VMEM((2, STEPS, 8, 8, 256), f32),
            pltpu.VMEM((2, 8, 8, 256), f32),
            pltpu.VMEM((2, 8, 8, 256), f32),
            pltpu.VMEM((25, 8, 8, 256), f32),
            pltpu.VMEM((2, 16, 8, 128), f32),
            pltpu.VMEM((2, 8, 8, 128), f32),
            pltpu.VMEM((2, 8, 8, 128), f32),
            pltpu.VMEM((n_x, 2, 2, 256), f32),
            pltpu.VMEM((1, n_x), jnp.int32),
            pltpu.VMEM((STEPS, 8, 8), f32),
            pltpu.VMEM((2, 2), jnp.int32),
            pltpu.VMEM((STEPS, 8, 8, 128), f32),
            pltpu.VMEM((8, 8, 128), f32),
            pltpu.VMEM((8, 8, 128), f32),
            pltpu.VMEM((8, 8, 128), f32),
            pltpu.SemaphoreType.DMA((3,)),
            pltpu.SemaphoreType.DMA((3,)),
            pltpu.SemaphoreType.DMA((2,)),
            pltpu.SemaphoreType.DMA,
            pltpu.SemaphoreType.DMA((10,)),
            pltpu.SemaphoreType.DMA((11,)),
            pltpu.SemaphoreType.DMA((2, STEPS, 4)),
            pltpu.SemaphoreType.DMA((2, STEPS, 4)),
            pltpu.SemaphoreType.DMA((2,)),
            pltpu.SemaphoreType.DMA((5,)),
        ],
        compiler_params=pltpu.CompilerParams(
            collective_id=0, has_side_effects=True, vmem_limit_bytes=48 * 1024 * 1024
        ),
        cost_estimate=pl.CostEstimate(flops=8_000_000, bytes_accessed=800_000, transcendentals=0),
    )(velocity, density, stored, holders, adjoint, traces, aperture)


def solution(mesh):
    return jax.shard_map(
        functools.partial(shards, mesh.shape["gx"], mesh.shape["gy"]),
        mesh=mesh,
        in_specs=(
            P("gx", "gy", "shot"),
            P("gx", "gy", "shot"),
            P("gx", None, ("shot", "gy"), None),
            P("gx", None),
            P("shot", None, "gx", "gy", None),
            P("shot", None, "gx", "gy"),
            P(),
        ),
        out_specs=(
            P("gx", "gy", "shot"),
            P("shot", None, "gx", "gy", None),
            P("shot", None, "gx", "gy", None),
        ),
        check_vma=False,
    )
```

```python
import functools

import jax
import jax.numpy as jnp
from jax import lax
from jax.experimental import pallas as pl
from jax.experimental.pallas import tpu as pltpu
from jax.sharding import PartitionSpec as P

REC_Z = 8
STEPS = 4
LAPLACE_TAPS = (-205.0 / 72.0, 8.0 / 5.0, -1.0 / 5.0, 8.0 / 315.0, -1.0 / 560.0)
SLOPE_TAPS = (4.0 / 5.0, -1.0 / 5.0, 4.0 / 105.0, -1.0 / 280.0)


def y_plus(centre, halo, row, k):
    return pltpu.roll(jnp.where(row < k, halo, centre), 8 - k, 1)


def y_minus(centre, halo, row, k):
    return pltpu.roll(jnp.where(row >= 8 - k, halo, centre), k, 1)


def z_plus(lower, upper, lane, k):
    low, up = pltpu.roll(lower, 128 - k, 2), pltpu.roll(upper, 128 - k, 2)
    return jnp.where(lane < 128 - k, low, up), up


def z_minus(lower, upper, lane, k):
    low, up = pltpu.roll(lower, k, 2), pltpu.roll(upper, k, 2)
    return low, jnp.where(lane >= k, up, low)


def kernel(
    n_x,
    n_y,
    velocity,
    density,
    stored,
    holders,
    adjoint,
    traces,
    aperture,
    image_out,
    forward_out,
    adjoint_out,
    field,
    halo,
    before,
    last,
    coef,
    dens,
    dens_y,
    speed,
    pieces,
    holders_v,
    traces_v,
    aperture_v,
    inject,
    share,
    partner_share,
    small_sem,
    local_sem,
    own_sem,
    piece_sem,
    model_sem,
    send_sem,
    halo_send,
    halo_recv,
    image_sem,
    out_sem,
):
    s, b, j = lax.axis_index("shot"), lax.axis_index("gx"), lax.axis_index("gy")
    other = 1 - s
    right, left = lax.rem(b + 1, n_x), lax.rem(b + n_x - 1, n_x)
    up, down = lax.rem(j + 1, n_y), lax.rem(j + n_y - 1, n_y)

    smalls = [
        pltpu.make_async_copy(holders, holders_v, small_sem.at[0]),
        pltpu.make_async_copy(traces.at[0], traces_v, small_sem.at[1]),
        pltpu.make_async_copy(aperture, aperture_v, small_sem.at[2]),
    ]
    owns = [
        pltpu.make_async_copy(adjoint.at[0, 0], field.at[1, 0, pl.ds(4, 8)], own_sem.at[0]),
        pltpu.make_async_copy(adjoint.at[0, 1], before.at[1], own_sem.at[1]),
    ]
    own_model = [
        pltpu.make_async_copy(density, dens.at[s, pl.ds(4, 8)], local_sem.at[0]),
        pltpu.make_async_copy(velocity, speed.at[s], local_sem.at[1]),
        pltpu.make_async_copy(stored.at[b], pieces.at[b], local_sem.at[2]),
    ]
    for copy in smalls + owns + own_model:
        copy.start()

    @pl.when(b == 0)
    def _():
        field[:, :, :4] = jnp.zeros((2, STEPS, 4, 8, 256), jnp.float32)
        dens[:, :4] = jnp.ones((2, 4, 8, 128), jnp.float32)

    @pl.when(b == n_x - 1)
    def _():
        field[:, :, 12:] = jnp.zeros((2, STEPS, 4, 8, 256), jnp.float32)
        dens[:, 12:] = jnp.ones((2, 4, 8, 128), jnp.float32)

    @pl.when(j == 0)
    def _():
        halo[:, :, :, 4:] = jnp.zeros((2, STEPS, 8, 4, 256), jnp.float32)
        dens_y[:, :, 4:] = jnp.ones((2, 8, 4, 128), jnp.float32)

    @pl.when(j == n_y - 1)
    def _():
        halo[:, :, :, :4] = jnp.zeros((2, STEPS, 8, 4, 256), jnp.float32)
        dens_y[:, :, :4] = jnp.ones((2, 8, 4, 128), jnp.float32)

    barrier = pltpu.get_barrier_semaphore()

    def greet(step, carry):
        pl.semaphore_signal(barrier, inc=1, device_id={"gx": lax.rem(b + step, n_x)})
        return carry

    lax.fori_loop(1, n_x, greet, 0)
    near = [
        {"shot": other},
        {"shot": other, "gx": right},
        {"shot": other, "gx": left},
        {"gy": up},
        {"gy": down},
        {"shot": other, "gy": up},
        {"shot": other, "gy": down},
    ]
    for target in near:
        pl.semaphore_signal(barrier, inc=1, device_id=target)
    pl.semaphore_wait(barrier, n_x - 1 + len(near))

    def send_piece(step, carry):
        target = lax.rem(b + step, n_x)
        pltpu.make_async_remote_copy(
            stored.at[target], pieces.at[b], send_sem.at[0], piece_sem, device_id={"gx": target}
        ).start()
        return carry

    lax.fori_loop(1, n_x, send_piece, 0)

    first_x, last_x = b == 0, b == n_x - 1
    first_y, last_y = j == 0, j == n_y - 1
    sends_to = [jnp.logical_not(edge) for edge in (last_x, first_x, first_y, last_y)]
    gets_from = [jnp.logical_not(edge) for edge in (first_x, last_x, last_y, first_y)]

    def start_all(copies, sides):
        for copy, side in zip(copies, sides):
            pl.when(sends_to[side])(copy.start)

    def recv_all(copies, sides):
        for copy, side in zip(copies, sides):
            pl.when(gets_from[side])(copy.wait_recv)

    def sent_all(copies, sides):
        for copy, side in zip(copies, sides):
            pl.when(sends_to[side])(copy.wait_send)

    def halo_sends(which, level, source):
        edges = [
            (source(pl.ds(4, 4), None), field.at[which, level, pl.ds(0, 4)], {"gx": right}),
            (source(pl.ds(0, 4), None), field.at[which, level, pl.ds(12, 4)], {"gx": left}),
            (source(pl.ds(0, 8), pl.ds(0, 4)), halo.at[which, level, :, pl.ds(0, 4)], {"gy": down}),
            (source(pl.ds(0, 8), pl.ds(4, 4)), halo.at[which, level, :, pl.ds(4, 4)], {"gy": up}),
        ]
        copies = []
        for side, (src, dst, target) in enumerate(edges):
            copies.append(
                pltpu.make_async_remote_copy(
                    src,
                    dst,
                    halo_send.at[which, level, side],
                    halo_recv.at[which, level, side],
                    device_id=target,
                )
            )
        start_all(copies, range(4))
        return copies

    def from_argument(planes, rows):
        return adjoint.at[0, 0, planes] if rows is None else adjoint.at[0, 0, planes, rows]

    def from_field(which, level):
        def source(planes, rows):
            planes = pl.ds(planes.start + 4, planes.size)
            if rows is None:
                return field.at[which, level, planes]
            return field.at[which, level, planes, rows]

        return source

    sends = {(1, 0): halo_sends(1, 0, from_argument)}

    model = [
        (velocity, speed.at[s], {"shot": other}),
        (density, dens.at[s, pl.ds(4, 8)], {"shot": other}),
    ]
    for place in (s, other):
        model += [
            (density.at[pl.ds(4, 4)], dens.at[s, pl.ds(0, 4)], {"shot": place, "gx": right}),
            (density.at[pl.ds(0, 4)], dens.at[s, pl.ds(12, 4)], {"shot": place, "gx": left}),
            (density.at[:, pl.ds(0, 4)], dens_y.at[s, :, pl.ds(0, 4)], {"shot": place, "gy": down}),
            (density.at[:, pl.ds(4, 4)], dens_y.at[s, :, pl.ds(4, 4)], {"shot": place, "gy": up}),
        ]
    model_copies = []
    for at, (src, dst, target) in enumerate(model):
        model_copies.append(
            pltpu.make_async_remote_copy(
                src, dst, send_sem.at[1 + at], model_sem.at[at], device_id=target
            )
        )
    for copy in model_copies[:2]:
        copy.start()
    start_all(model_copies[2:], (0, 1, 2, 3) * 2)

    row = lax.broadcasted_iota(jnp.int32, (8, 8, 128), 1)
    lane = lax.broadcasted_iota(jnp.int32, (8, 8, 128), 2)
    low, high = pl.ds(0, 128), pl.ds(128, 128)

    for copy in smalls:
        copy.wait()
    column = lax.broadcasted_iota(jnp.int32, (64, n_x), 0)
    place = column // 2
    parity = column - 2 * place
    hit = holders_v[...] == place
    picks = [jnp.where(hit & (parity == r), 1.0, 0.0).astype(jnp.float32) for r in range(2)]

    bounds = aperture_v[...]
    bounds = jnp.where(s == 0, bounds[0:1], bounds[1:2])
    active = jnp.where((b >= bounds[:, 0:1]) & (b < bounds[:, 1:2]), 1.0, 0.0).astype(jnp.float32)
    active = active.reshape(1, 1, 1)

    for copy in own_model[:2]:
        copy.wait()
    for copy in model_copies[:2]:
        copy.wait_recv()
    recv_all(model_copies[2:], (0, 1, 2, 3) * 2)

    keep_left = jnp.where(first_x, 0.0, 1.0).astype(jnp.float32)
    keep_right = jnp.where(last_x, 0.0, 1.0).astype(jnp.float32)
    keep_down = jnp.where(first_y, 0.0, 1.0).astype(jnp.float32)
    keep_up = jnp.where(last_y, 0.0, 1.0).astype(jnp.float32)
    logs, logs_y = [], []
    for half in range(2):
        wide = jnp.log(dens[half])
        logs.append(
            jnp.concatenate([wide[:4] * keep_left, wide[4:12], wide[12:] * keep_right], axis=0)
        )
        logs_y.append(jnp.log(dens_y[half]) * jnp.where(row < 4, keep_up, keep_down))
    inner = [logs[half][4:12] for half in range(2)]
    grad_x, grad_y, grad_z = [0.0, 0.0], [0.0, 0.0], [0.0, 0.0]
    for k in range(1, 5):
        tap = SLOPE_TAPS[k - 1]
        ahead = z_plus(inner[0], inner[1], lane, k)
        behind = z_minus(inner[0], inner[1], lane, k)
        ahead = (ahead[0], jnp.where(lane < 128 - k, ahead[1], 0.0))
        behind = (jnp.where(lane >= k, behind[0], 0.0), behind[1])
        for half in range(2):
            wide = logs[half]
            grad_x[half] += tap * (wide[4 + k : 12 + k] - wide[4 - k : 12 - k])
            grad_y[half] += tap * (
                y_plus(inner[half], logs_y[half], row, k)
                - y_minus(inner[half], logs_y[half], row, k)
            )
            grad_z[half] += tap * (ahead[half] - behind[half])

    for half, lanes in enumerate((low, high)):
        root = speed[half]
        sq = root * root
        coef[0, :, :, lanes] = 2.0 + (3.0 * LAPLACE_TAPS[0]) * sq
        for k in range(1, 5):
            even = LAPLACE_TAPS[k] * sq
            at = 1 + 6 * (k - 1)
            odd = SLOPE_TAPS[k - 1] * (sq * grad_x[half])
            plus, minus = even - odd, even + odd
            coef[at, : 8 - k, :, lanes] = plus[: 8 - k]
            coef[at, 8 - k :, :, lanes] = plus[8 - k :] * keep_right
            coef[at + 1, :k, :, lanes] = minus[:k] * keep_left
            coef[at + 1, k:, :, lanes] = minus[k:]
            odd = SLOPE_TAPS[k - 1] * (sq * grad_y[half])
            coef[at + 2, :, :, lanes] = (even - odd) * jnp.where(row >= 8 - k, keep_up, 1.0)
            coef[at + 3, :, :, lanes] = (even + odd) * jnp.where(row < k, keep_down, 1.0)
            odd = SLOPE_TAPS[k - 1] * (sq * grad_z[half])
            plus, minus = even - odd, even + odd
            if half == 0:
                minus = jnp.where(lane >= k, minus, 0.0)
            else:
                plus = jnp.where(lane < 128 - k, plus, 0.0)
            coef[at + 4, :, :, lanes] = plus
            coef[at + 5, :, :, lanes] = minus
        if half == 0:
            eye = lax.broadcasted_iota(jnp.int32, (8, 8), 0) == lax.broadcasted_iota(
                jnp.int32, (8, 8), 1
            )
            at_receiver = lax.broadcasted_iota(jnp.int32, (8, 128), 1) == REC_Z
            for number in range(STEPS):
                for x in range(8):
                    line = jnp.where(eye, traces_v[number, pl.ds(x, 1), :], 0.0)
                    line = jnp.sum(line, axis=1, keepdims=True)
                    inject[number, x] = jnp.where(at_receiver, line, 0.0) * sq[x]

    def advance(which, level):
        previous = before.at[which] if level == 0 else field.at[which, level - 1, pl.ds(4, 8)]
        wide = field.at[which, level]
        centre = [wide[4:12, :, lanes] for lanes in (low, high)]
        edge = [halo[which, level, :, :, lanes] for lanes in (low, high)]
        total = [
            coef[0, :, :, lanes] * centre[half] - previous[:, :, lanes]
            for half, lanes in enumerate((low, high))
        ]
        for k in range(1, 5):
            at = 1 + 6 * (k - 1)
            ahead = z_plus(centre[0], centre[1], lane, k)
            behind = z_minus(centre[0], centre[1], lane, k)
            for half, lanes in enumerate((low, high)):
                total[half] = (
                    total[half]
                    + coef[at, :, :, lanes] * wide[4 + k : 12 + k, :, lanes]
                    + coef[at + 1, :, :, lanes] * wide[4 - k : 12 - k, :, lanes]
                    + coef[at + 2, :, :, lanes] * y_plus(centre[half], edge[half], row, k)
                    + coef[at + 3, :, :, lanes] * y_minus(centre[half], edge[half], row, k)
                    + coef[at + 4, :, :, lanes] * ahead[half]
                    + coef[at + 5, :, :, lanes] * behind[half]
                )
        if which == 1:
            total[0] = total[0] + inject[STEPS - 1 - level]
        return total

    def step(which, level):
        recv_all(sends[which, level], range(4))
        new = advance(which, level)
        if level == STEPS - 1:
            for half, lanes in enumerate((low, high)):
                last[which, :, :, lanes] = new[half]
            return
        for half, lanes in enumerate((low, high)):
            field[which, level + 1, 4:12, :, lanes] = new[half]
        sends[which, level + 1] = halo_sends(which, level + 1, from_field(which, level + 1))

    for copy in owns:
        copy.wait()
    step(1, 0)

    own_model[2].wait()
    pltpu.make_async_copy(pieces.at[pl.ds(0, n_x - 1)], pieces.at[pl.ds(0, n_x - 1)], piece_sem).wait()
    for level in (0, 1):
        found = 0.0
        for r in range(2):
            found += jnp.dot(
                picks[r],
                pieces[:, level, r, :],
                precision=lax.Precision.HIGHEST,
                preferred_element_type=jnp.float32,
            )
        found = found.reshape(8, 8, 256)
        if level == 0:
            field[0, 0, 4:12] = found
            sends[0, 0] = halo_sends(0, 0, from_field(0, 0))
        else:
            before[0] = found

    step(1, 1)
    step(0, 0)
    step(1, 2)
    outs = [
        pltpu.make_async_copy(field.at[1, 3, pl.ds(4, 8)], adjoint_out.at[0, 1], out_sem.at[0])
    ]
    outs[0].start()
    step(0, 1)
    step(1, 3)
    outs.append(pltpu.make_async_copy(last.at[1], adjoint_out.at[0, 0], out_sem.at[1]))
    outs[1].start()
    step(0, 2)
    outs.append(
        pltpu.make_async_copy(field.at[0, 3, pl.ds(4, 8)], forward_out.at[0, 1], out_sem.at[2])
    )
    outs[2].start()
    early = [0.0, 0.0]
    for number in range(1, STEPS):
        for half, lanes in enumerate((low, high)):
            early[half] += (
                field[0, number, 4:12, :, lanes] * field[1, STEPS - number, 4:12, :, lanes]
            )
    step(0, 3)
    outs.append(pltpu.make_async_copy(last.at[0], forward_out.at[0, 0], out_sem.at[3]))
    outs[3].start()
    whole = [
        active * (early[half] + last[0, :, :, lanes] * field[1, 0, 4:12, :, lanes])
        for half, lanes in enumerate((low, high))
    ]
    share[...] = jnp.where(s == 0, whole[1], whole[0])
    to_partner = pltpu.make_async_remote_copy(
        share, partner_share, image_sem.at[0], image_sem.at[1], device_id={"shot": other}
    )
    to_partner.start()
    mine = jnp.where(s == 0, whole[0], whole[1])

    pltpu.make_async_copy(
        stored.at[pl.ds(0, n_x - 1)], stored.at[pl.ds(0, n_x - 1)], send_sem.at[0]
    ).wait()
    for copy in model_copies[:2]:
        copy.wait_send()
    sent_all(model_copies[2:], (0, 1, 2, 3) * 2)
    for copies in sends.values():
        sent_all(copies, range(4))

    to_partner.wait()
    image_out[...] = mine + partner_share[...]
    for copy in outs:
        copy.wait()


def finish(image, forward, adjoint, image_out, forward_out, adjoint_out, sem):
    copies = [
        pltpu.make_async_copy(src, dst, sem.at[at])
        for at, (src, dst) in enumerate(
            ((image, image_out), (forward, forward_out), (adjoint, adjoint_out))
        )
    ]
    for copy in copies:
        copy.start()
    for copy in copies:
        copy.wait()


def shards(n_x, n_y, velocity, density, stored, holders, adjoint, traces, aperture):
    f32 = jnp.float32
    anywhere = pl.BlockSpec(memory_space=pl.ANY)
    inside = pl.BlockSpec(memory_space=pltpu.VMEM)
    results = pl.pallas_call(
        functools.partial(kernel, n_x, n_y),
        out_shape=(
            pltpu.VMEM((8, 8, 128), f32),
            pltpu.VMEM((1, 2, 8, 8, 256), f32),
            pltpu.VMEM((1, 2, 8, 8, 256), f32),
        ),
        in_specs=[anywhere] * 7,
        out_specs=(inside,) * 3,
        scratch_shapes=[
            pltpu.VMEM((2, STEPS, 16, 8, 256), f32),
            pltpu.VMEM((2, STEPS, 8, 8, 256), f32),
            pltpu.VMEM((2, 8, 8, 256), f32),
            pltpu.VMEM((2, 8, 8, 256), f32),
            pltpu.VMEM((25, 8, 8, 256), f32),
            pltpu.VMEM((2, 16, 8, 128), f32),
            pltpu.VMEM((2, 8, 8, 128), f32),
            pltpu.VMEM((2, 8, 8, 128), f32),
            pltpu.VMEM((n_x, 2, 2, 256), f32),
            pltpu.VMEM((1, n_x), jnp.int32),
            pltpu.VMEM((STEPS, 8, 8), f32),
            pltpu.VMEM((2, 2), jnp.int32),
            pltpu.VMEM((STEPS, 8, 8, 128), f32),
            pltpu.VMEM((8, 8, 128), f32),
            pltpu.VMEM((8, 8, 128), f32),
            pltpu.SemaphoreType.DMA((3,)),
            pltpu.SemaphoreType.DMA((3,)),
            pltpu.SemaphoreType.DMA((2,)),
            pltpu.SemaphoreType.DMA,
            pltpu.SemaphoreType.DMA((10,)),
            pltpu.SemaphoreType.DMA((11,)),
            pltpu.SemaphoreType.DMA((2, STEPS, 4)),
            pltpu.SemaphoreType.DMA((2, STEPS, 4)),
            pltpu.SemaphoreType.DMA((2,)),
            pltpu.SemaphoreType.DMA((4,)),
        ],
        compiler_params=pltpu.CompilerParams(
            collective_id=0, has_side_effects=True, vmem_limit_bytes=48 * 1024 * 1024
        ),
        cost_estimate=pl.CostEstimate(flops=8_000_000, bytes_accessed=800_000, transcendentals=0),
    )(*(
        pltpu.with_memory_space_constraint(given, pltpu.HBM)
        for given in (velocity, density, stored, holders, adjoint, traces, aperture)
    ))
    return pl.pallas_call(
        finish,
        out_shape=tuple(jax.ShapeDtypeStruct(one.shape, f32) for one in results),
        in_specs=[inside] * 3,
        out_specs=(anywhere,) * 3,
        scratch_shapes=[pltpu.SemaphoreType.DMA((3,))],
    )(*(pltpu.with_memory_space_constraint(one, pltpu.VMEM) for one in results))


def solution(mesh):
    return jax.shard_map(
        functools.partial(shards, mesh.shape["gx"], mesh.shape["gy"]),
        mesh=mesh,
        in_specs=(
            P("gx", "gy", "shot"),
            P("gx", "gy", "shot"),
            P("gx", None, ("shot", "gy"), None),
            P("gx", None),
            P("shot", None, "gx", "gy", None),
            P("shot", None, "gx", "gy"),
            P(),
        ),
        out_specs=(
            P("gx", "gy", "shot"),
            P("shot", None, "gx", "gy", None),
            P("shot", None, "gx", "gy", None),
        ),
        check_vma=False,
    )
```

```python
import functools

import jax
import jax.numpy as jnp
from jax import lax
from jax.experimental import pallas as pl
from jax.experimental.pallas import tpu as pltpu
from jax.sharding import PartitionSpec as P

REC_Z = 8
STEPS = 4
LAPLACE_TAPS = (-205.0 / 72.0, 8.0 / 5.0, -1.0 / 5.0, 8.0 / 315.0, -1.0 / 560.0)
SLOPE_TAPS = (4.0 / 5.0, -1.0 / 5.0, 4.0 / 105.0, -1.0 / 280.0)


def y_plus(centre, halo, row, k):
    return pltpu.roll(jnp.where(row < k, halo, centre), 8 - k, 1)


def y_minus(centre, halo, row, k):
    return pltpu.roll(jnp.where(row >= 8 - k, halo, centre), k, 1)


def z_plus(lower, upper, lane, k):
    low, up = pltpu.roll(lower, 128 - k, 2), pltpu.roll(upper, 128 - k, 2)
    return jnp.where(lane < 128 - k, low, up), up


def z_minus(lower, upper, lane, k):
    low, up = pltpu.roll(lower, k, 2), pltpu.roll(upper, k, 2)
    return low, jnp.where(lane >= k, up, low)


def y_plus_outer(centre, above, below, row, k):
    return pltpu.roll(jnp.where(row < k, centre, jnp.where(row < k + 4, above, below)), 8 - k, 1)


def y_minus_outer(centre, above, below, row, k):
    return pltpu.roll(
        jnp.where(row >= 8 - k, centre, jnp.where(row < 4 - k, above, below)), k, 1
    )


def kernel(
    n_x,
    n_y,
    velocity,
    density,
    stored,
    holders,
    adjoint,
    traces,
    aperture,
    image_out,
    forward_out,
    adjoint_out,
    wide,
    below,
    above,
    corner,
    ring,
    mid,
    mid_y,
    old,
    old_y,
    back,
    back_y,
    back_old,
    last,
    coef,
    coef_y,
    dens,
    dens_below,
    dens_above,
    dens_corner,
    speed,
    speed_y,
    pieces,
    holders_v,
    traces_v,
    aperture_v,
    inject,
    share,
    partner_share,
    small_sem,
    local_sem,
    own_sem,
    piece_sem,
    piece_send,
    model_send,
    model_recv,
    deep_send,
    deep_recv,
    old_send,
    old_recv,
    back_send,
    back_recv,
    image_sem,
    out_sem,
):
    s, b, j = lax.axis_index("shot"), lax.axis_index("gx"), lax.axis_index("gy")
    other = 1 - s
    f32 = jnp.float32

    smalls = [
        pltpu.make_async_copy(holders, holders_v, small_sem.at[0]),
        pltpu.make_async_copy(traces.at[0], traces_v, small_sem.at[1]),
        pltpu.make_async_copy(aperture, aperture_v, small_sem.at[2]),
    ]
    owns = [
        pltpu.make_async_copy(adjoint.at[0, 0], back.at[0, pl.ds(4, 8)], own_sem.at[0]),
        pltpu.make_async_copy(adjoint.at[0, 1], back_old, own_sem.at[1]),
    ]
    own_model = [
        pltpu.make_async_copy(density, dens.at[s, pl.ds(8, 8)], local_sem.at[0]),
        pltpu.make_async_copy(velocity, speed.at[s, pl.ds(4, 8)], local_sem.at[1]),
        pltpu.make_async_copy(stored.at[b], pieces.at[b], local_sem.at[2]),
    ]

    barrier = pltpu.get_barrier_semaphore()

    def greet(step, carry):
        pl.semaphore_signal(barrier, inc=1, device_id={"gx": lax.rem(b + step, n_x)})
        return carry

    lax.fori_loop(1, n_x, greet, 0)

    def toward(dx, dy, shot=None):
        target = {} if shot is None else {"shot": shot}
        if dx:
            target["gx"] = lax.rem(b + n_x + dx, n_x)
        if dy:
            target["gy"] = lax.rem(j + n_y + dy, n_y)
        return target

    sides = ((1, 0), (-1, 0), (0, 1), (0, -1))
    diagonals = ((1, 1), (1, -1), (-1, 1), (-1, -1))
    near = [{"shot": other}]
    near += [toward(0, dy) for dy in (1, -1)]
    near += [toward(dx, dy) for dx, dy in diagonals]
    near += [toward(dx, dy, other) for dx, dy in sides + diagonals]
    for target in near:
        pl.semaphore_signal(barrier, inc=1, device_id=target)

    for copy in own_model + owns + smalls:
        copy.start()

    def fill(refs, value):
        for ref in refs:
            ref[...] = jnp.full(ref.shape, value, f32)

    @pl.when(b == 0)
    def _():
        fill((wide.at[:, :8], corner.at[:, :4], old.at[:4], back.at[:, :4], speed.at[:, :4]), 0.0)
        fill((dens.at[:, :8], dens_corner.at[:, :4]), 1.0)

    @pl.when(b == n_x - 1)
    def _():
        fill((wide.at[:, 16:], corner.at[:, 4:], old.at[12:], back.at[:, 12:], speed.at[:, 12:]), 0.0)
        fill((dens.at[:, 16:], dens_corner.at[:, 4:]), 1.0)

    @pl.when(j == 0)
    def _():
        fill((below, corner.at[:, :, 4:], old_y.at[:, 4:], back_y.at[:, :, 4:], speed_y.at[:, :, 4:]), 0.0)
        fill((dens_below, dens_corner.at[:, :, 4:]), 1.0)

    @pl.when(j == n_y - 1)
    def _():
        fill((above, corner.at[:, :, :4], old_y.at[:, :4], back_y.at[:, :, :4], speed_y.at[:, :, :4]), 0.0)
        fill((dens_above, dens_corner.at[:, :, :4]), 1.0)

    pl.semaphore_wait(barrier, n_x - 1 + len(near))

    def send_piece(step, carry):
        target = lax.rem(b + step, n_x)
        pltpu.make_async_remote_copy(
            stored.at[target], pieces.at[b], piece_send, piece_sem, device_id={"gx": target}
        ).start()
        return carry

    lax.fori_loop(1, n_x, send_piece, 0)

    def exists(dx, dy):
        there = b >= 0
        if dx:
            there &= (b < n_x - 1) if dx > 0 else (b > 0)
        if dy:
            there &= (j < n_y - 1) if dy > 0 else (j > 0)
        return there

    class Group:
        def __init__(self, entries, send_sem, recv_sem):
            self.items = []
            for at, (dx, dy, shot, src, dst) in enumerate(entries):
                copy = pltpu.make_async_remote_copy(
                    src, dst, send_sem.at[at], recv_sem.at[at], device_id=toward(dx, dy, shot)
                )
                self.items.append((copy, dx, dy))
            for copy, dx, dy in self.items:
                self.guard(dx, dy, copy.start)

        def guard(self, dx, dy, action):
            if dx or dy:
                pl.when(exists(dx, dy))(action)
            else:
                action()

        def received(self):
            for copy, dx, dy in self.items:
                self.guard(-dx, -dy, copy.wait_recv)

        def sent(self):
            for copy, dx, dy in self.items:
                self.guard(dx, dy, copy.wait_send)

    first, final = pl.ds(0, 4), pl.ds(4, 4)

    def shallow(src, base, planes, rows, shot=None):
        return [
            (1, 0, shot, src.at[pl.ds(base + 4, 4)], planes.at[pl.ds(0, 4)]),
            (-1, 0, shot, src.at[pl.ds(base, 4)], planes.at[pl.ds(12, 4)]),
            (0, 1, shot, src.at[pl.ds(base, 8), final], rows.at[:, final]),
            (0, -1, shot, src.at[pl.ds(base, 8), first], rows.at[:, first]),
        ]

    def deep(src, base, planes, lower, upper, corners, shot=None):
        whole = src.at[pl.ds(base, 8)]
        entries = [
            (1, 0, shot, whole, planes.at[pl.ds(0, 8)]),
            (-1, 0, shot, whole, planes.at[pl.ds(16, 8)]),
            (0, 1, shot, whole, lower),
            (0, -1, shot, whole, upper),
        ]
        for dx, dy in diagonals:
            rows = final if dy > 0 else first
            here = pl.ds(base + 4, 4) if dx > 0 else pl.ds(base, 4)
            there = first if dx > 0 else final
            entries.append((dx, dy, shot, src.at[here, rows], corners.at[there, rows]))
        return entries

    model = [
        (0, 0, other, density, dens.at[s, pl.ds(8, 8)]),
        (0, 0, other, velocity, speed.at[s, pl.ds(4, 8)]),
    ]
    for shot in (s, other):
        model += deep(
            density, 0, dens.at[s], dens_below.at[s], dens_above.at[s], dens_corner.at[s], shot
        )
        model += shallow(velocity, 0, speed.at[s], speed_y.at[s], shot)
    model = Group(model, model_send, model_recv)
    groups = [model]
    backs = [
        Group(
            shallow(adjoint.at[0, 0], 0, back.at[0], back_y.at[0]), back_send.at[0], back_recv.at[0]
        )
    ]

    row = lax.broadcasted_iota(jnp.int32, (1, 8, 128), 1)
    lane = lax.broadcasted_iota(jnp.int32, (1, 8, 128), 2)
    halves = (pl.ds(0, 128), pl.ds(128, 128))

    for copy in smalls:
        copy.wait()
    column = lax.broadcasted_iota(jnp.int32, (64, n_x), 0)
    place = column // 2
    parity = column - 2 * place
    hit = holders_v[...] == place
    picks = [jnp.where(hit & (parity == r), 1.0, 0.0).astype(f32) for r in range(2)]

    bounds = aperture_v[...]
    bounds = jnp.where(s == 0, bounds[0:1], bounds[1:2])
    active = jnp.where((b >= bounds[:, 0:1]) & (b < bounds[:, 1:2]), 1.0, 0.0).astype(f32)
    active = active.reshape(1, 1, 1)

    for copy in own_model[:2]:
        copy.wait()
    model.received()

    for half in range(2):
        dens[half] = jnp.log(dens[half])
        dens_below[half] = jnp.log(dens_below[half])
        dens_above[half] = jnp.log(dens_above[half])
        dens_corner[half] = jnp.log(dens_corner[half])

    def coefficients(out, count, speeds, logs, x_of, plus_of, minus_of):
        grads = [[0.0, 0.0, 0.0] for half in range(2)]
        for k in range(1, 5):
            tap = SLOPE_TAPS[k - 1]
            ahead = z_plus(logs[0], logs[1], lane, k)
            behind = z_minus(logs[0], logs[1], lane, k)
            ahead = (ahead[0], jnp.where(lane < 128 - k, ahead[1], 0.0))
            behind = (jnp.where(lane >= k, behind[0], 0.0), behind[1])
            for half in range(2):
                grads[half][0] += tap * (x_of(half, k) - x_of(half, -k))
                grads[half][1] += tap * (plus_of(half, k) - minus_of(half, k))
                grads[half][2] += tap * (ahead[half] - behind[half])
        for half, lanes in enumerate(halves):
            sq = speeds(half)
            sq = sq * sq
            out[0, :, :, lanes] = 2.0 + (3.0 * LAPLACE_TAPS[0]) * sq
            slopes = [sq * grad for grad in grads[half]]
            for k in range(1, 5):
                even = LAPLACE_TAPS[k] * sq
                for axis in range(3):
                    odd = SLOPE_TAPS[k - 1] * slopes[axis]
                    plus, minus = even - odd, even + odd
                    if axis == 2 and half == 0:
                        minus = jnp.where(lane >= k, minus, 0.0)
                    elif axis == 2:
                        plus = jnp.where(lane < 128 - k, plus, 0.0)
                    at = 1 + 6 * (k - 1) + 2 * axis
                    out[at, :, :, lanes] = plus
                    out[at + 1, :, :, lanes] = minus

    def ring_of(half):
        inner = jnp.where(row < 4, dens_above[half], dens_below[half])
        return jnp.concatenate([dens_corner[half, :4], inner, dens_corner[half, 4:]], axis=0)

    rings = [ring_of(half) for half in range(2)]
    coefficients(
        coef,
        16,
        lambda half: speed[half],
        [dens[half, 4:20] for half in range(2)],
        lambda half, k: dens[half, 4 + k : 20 + k],
        lambda half, k: y_plus(dens[half, 4:20], rings[half], row, k),
        lambda half, k: y_minus(dens[half, 4:20], rings[half], row, k),
    )

    eye = lax.broadcasted_iota(jnp.int32, (8, 8), 0) == lax.broadcasted_iota(jnp.int32, (8, 8), 1)
    at_receiver = lax.broadcasted_iota(jnp.int32, (8, 128), 1) == REC_Z
    for x in range(8):
        sq = speed[0, 4 + x] * speed[0, 4 + x]
        for number in range(STEPS):
            line = jnp.where(eye, traces_v[number, pl.ds(x, 1), :], 0.0)
            line = jnp.sum(line, axis=1, keepdims=True)
            inject[number, x] = jnp.where(at_receiver, line, 0.0) * sq

    def taps(table, planes, centre, x_of, plus_of, minus_of, before):
        total = [
            table[0, planes, :, lanes] * centre[half] - before[half]
            for half, lanes in enumerate(halves)
        ]
        for k in range(1, 5):
            at = 1 + 6 * (k - 1)
            ahead = z_plus(centre[0], centre[1], lane, k)
            behind = z_minus(centre[0], centre[1], lane, k)
            for half, lanes in enumerate(halves):
                total[half] = (
                    total[half]
                    + table[at, planes, :, lanes] * x_of(half, k)
                    + table[at + 1, planes, :, lanes] * x_of(half, -k)
                    + table[at + 2, planes, :, lanes] * plus_of(half, k)
                    + table[at + 3, planes, :, lanes] * minus_of(half, k)
                    + table[at + 4, planes, :, lanes] * ahead[half]
                    + table[at + 5, planes, :, lanes] * behind[half]
                )
        return total

    def block(ref, low, count):
        return [ref[low : low + count, :, lanes] for lanes in halves]

    def inner_step(planes, rows, before):
        centre, edge = block(planes, 4, 8), block(rows, 0, 8)
        return taps(
            coef,
            slice(4, 12),
            centre,
            lambda half, k: planes[4 + k : 12 + k, :, halves[half]],
            lambda half, k: y_plus(centre[half], edge[half], row, k),
            lambda half, k: y_minus(centre[half], edge[half], row, k),
            before,
        )

    def back_step(level):
        backs[level].received()
        before = block(back_old, 0, 8) if level == 0 else block(back.at[level - 1], 4, 8)
        new = inner_step(back.at[level], back_y.at[level], before)
        new[0] = new[0] + inject[STEPS - 1 - level]
        if level == STEPS - 1:
            for half, lanes in enumerate(halves):
                last[1, :, :, lanes] = new[half]
            return
        for half, lanes in enumerate(halves):
            back[level + 1, 4:12, :, lanes] = new[half]
        backs.append(
            Group(
                shallow(back.at[level + 1], 4, back.at[level + 1], back_y.at[level + 1]),
                back_send.at[level + 1],
                back_recv.at[level + 1],
            )
        )

    for copy in owns:
        copy.wait()
    back_step(0)

    coefficients(
        coef_y,
        8,
        lambda half: speed_y[half],
        [rings[half][4:12] for half in range(2)],
        lambda half, k: rings[half][4 + k : 12 + k],
        lambda half, k: y_plus_outer(
            dens[half, 8:16], dens_above[half], dens_below[half], row, k
        ),
        lambda half, k: y_minus_outer(
            dens[half, 8:16], dens_above[half], dens_below[half], row, k
        ),
    )

    def send_deep(level):
        group = Group(
            deep(
                wide.at[level],
                8,
                wide.at[level],
                below.at[level],
                above.at[level],
                corner.at[level],
            ),
            deep_send.at[level],
            deep_recv.at[level],
        )
        groups.append(group)
        return group

    own_model[2].wait()
    arrived = pieces.at[pl.ds(0, n_x - 1)]
    pltpu.make_async_copy(arrived, arrived, piece_sem).wait()
    for level in (0, 1):
        found = 0.0
        for r in range(2):
            found += jnp.dot(
                picks[r],
                pieces[:, level, r, :],
                precision=lax.Precision.HIGHEST,
                preferred_element_type=f32,
            )
        found = found.reshape(8, 8, 256)
        if level == 0:
            wide[0, 8:16] = found
            exchange = send_deep(0)
        else:
            old[4:12] = found
            old_group = Group(shallow(old, 4, old, old_y), old_send, old_recv)
            groups.append(old_group)

    def outer_step(level, before, before_y):
        planes, low, up = wide.at[level], below.at[level], above.at[level]
        for lanes in halves:
            ring[0:4, :, lanes] = corner[level, 0:4, :, lanes]
            ring[4:12, :, lanes] = jnp.where(row < 4, up[:, :, lanes], low[:, :, lanes])
            ring[12:16, :, lanes] = corner[level, 4:8, :, lanes]
        edge = block(ring, 4, 8)
        new = taps(
            coef_y,
            slice(0, 8),
            edge,
            lambda half, k: ring[4 + k : 12 + k, :, halves[half]],
            lambda half, k: y_plus_outer(
                planes[8:16, :, halves[half]], up[:, :, halves[half]], low[:, :, halves[half]], row, k
            ),
            lambda half, k: y_minus_outer(
                planes[8:16, :, halves[half]], up[:, :, halves[half]], low[:, :, halves[half]], row, k
            ),
            block(before_y, 0, 8),
        )
        for half, lanes in enumerate(halves):
            mid_y[level, :, :, lanes] = new[half]
        for start in (0, 8):
            centre, around = block(planes, 4 + start, 8), block(ring, start, 8)
            new = taps(
                coef,
                slice(start, start + 8),
                centre,
                lambda half, k: planes[4 + start + k : 12 + start + k, :, halves[half]],
                lambda half, k: y_plus(centre[half], around[half], row, k),
                lambda half, k: y_minus(centre[half], around[half], row, k),
                block(before, start, 8),
            )
            for half, lanes in enumerate(halves):
                mid[level, start : start + 8, :, lanes] = new[half]

    back_step(1)
    exchange.received()
    old_group.received()
    outer_step(0, old, old_y)
    new = inner_step(mid.at[0], mid_y.at[0], block(wide.at[0], 8, 8))
    for half, lanes in enumerate(halves):
        wide[1, 8:16, :, lanes] = new[half]
    exchange = send_deep(1)

    back_step(2)
    outs = [pltpu.make_async_copy(back.at[3, pl.ds(4, 8)], adjoint_out.at[0, 1], out_sem.at[0])]
    outs[0].start()
    early = [
        mid[0, 4:12, :, lanes] * back[3, 4:12, :, lanes]
        + wide[1, 8:16, :, lanes] * back[2, 4:12, :, lanes]
        for lanes in halves
    ]

    exchange.received()
    outer_step(1, mid.at[0], mid_y.at[0])
    outs.append(
        pltpu.make_async_copy(mid.at[1, pl.ds(4, 8)], forward_out.at[0, 1], out_sem.at[1])
    )
    outs[1].start()
    new = inner_step(mid.at[1], mid_y.at[1], block(wide.at[1], 8, 8))
    whole = [
        active
        * (
            early[half]
            + mid[1, 4:12, :, lanes] * back[1, 4:12, :, lanes]
            + new[half] * back[0, 4:12, :, lanes]
        )
        for half, lanes in enumerate(halves)
    ]
    share[...] = jnp.where(s == 0, whole[1], whole[0])
    to_partner = pltpu.make_async_remote_copy(
        share, partner_share, image_sem.at[0], image_sem.at[1], device_id={"shot": other}
    )
    to_partner.start()
    for half, lanes in enumerate(halves):
        last[0, :, :, lanes] = new[half]
    outs.append(pltpu.make_async_copy(last.at[0], forward_out.at[0, 0], out_sem.at[2]))
    outs[2].start()
    image_out[...] = jnp.where(s == 0, whole[0], whole[1])

    back_step(3)
    outs.append(pltpu.make_async_copy(last.at[1], adjoint_out.at[0, 0], out_sem.at[3]))
    outs[3].start()

    gone = stored.at[pl.ds(0, n_x - 1)]
    pltpu.make_async_copy(gone, gone, piece_send).wait()
    for group in groups + backs:
        group.sent()

    to_partner.wait()
    image_out[...] += partner_share[...]
    for copy in outs:
        copy.wait()


def finish(image, forward, adjoint, image_out, forward_out, adjoint_out, sem):
    copies = [
        pltpu.make_async_copy(src, dst, sem.at[at])
        for at, (src, dst) in enumerate(
            ((image, image_out), (forward, forward_out), (adjoint, adjoint_out))
        )
    ]
    for copy in copies:
        copy.start()
    for copy in copies:
        copy.wait()


def shards(n_x, n_y, velocity, density, stored, holders, adjoint, traces, aperture):
    f32 = jnp.float32
    anywhere = pl.BlockSpec(memory_space=pl.ANY)
    inside = pl.BlockSpec(memory_space=pltpu.VMEM)
    results = pl.pallas_call(
        functools.partial(kernel, n_x, n_y),
        out_shape=(
            pltpu.VMEM((8, 8, 128), f32),
            pltpu.VMEM((1, 2, 8, 8, 256), f32),
            pltpu.VMEM((1, 2, 8, 8, 256), f32),
        ),
        in_specs=[anywhere] * 7,
        out_specs=(inside,) * 3,
        scratch_shapes=[
            pltpu.VMEM((2, 24, 8, 256), f32),
            pltpu.VMEM((2, 8, 8, 256), f32),
            pltpu.VMEM((2, 8, 8, 256), f32),
            pltpu.VMEM((2, 8, 8, 256), f32),
            pltpu.VMEM((16, 8, 256), f32),
            pltpu.VMEM((2, 16, 8, 256), f32),
            pltpu.VMEM((2, 8, 8, 256), f32),
            pltpu.VMEM((16, 8, 256), f32),
            pltpu.VMEM((8, 8, 256), f32),
            pltpu.VMEM((STEPS, 16, 8, 256), f32),
            pltpu.VMEM((STEPS, 8, 8, 256), f32),
            pltpu.VMEM((8, 8, 256), f32),
            pltpu.VMEM((2, 8, 8, 256), f32),
            pltpu.VMEM((25, 16, 8, 256), f32),
            pltpu.VMEM((25, 8, 8, 256), f32),
            pltpu.VMEM((2, 24, 8, 128), f32),
            pltpu.VMEM((2, 8, 8, 128), f32),
            pltpu.VMEM((2, 8, 8, 128), f32),
            pltpu.VMEM((2, 8, 8, 128), f32),
            pltpu.VMEM((2, 16, 8, 128), f32),
            pltpu.VMEM((2, 8, 8, 128), f32),
            pltpu.VMEM((n_x, 2, 2, 256), f32),
            pltpu.VMEM((1, n_x), jnp.int32),
            pltpu.VMEM((STEPS, 8, 8), f32),
            pltpu.VMEM((2, 2), jnp.int32),
            pltpu.VMEM((STEPS, 8, 8, 128), f32),
            pltpu.VMEM((8, 8, 128), f32),
            pltpu.VMEM((8, 8, 128), f32),
            pltpu.SemaphoreType.DMA((3,)),
            pltpu.SemaphoreType.DMA((3,)),
            pltpu.SemaphoreType.DMA((2,)),
            pltpu.SemaphoreType.DMA,
            pltpu.SemaphoreType.DMA,
            pltpu.SemaphoreType.DMA((26,)),
            pltpu.SemaphoreType.DMA((26,)),
            pltpu.SemaphoreType.DMA((2, 8)),
            pltpu.SemaphoreType.DMA((2, 8)),
            pltpu.SemaphoreType.DMA((4,)),
            pltpu.SemaphoreType.DMA((4,)),
            pltpu.SemaphoreType.DMA((STEPS, 4)),
            pltpu.SemaphoreType.DMA((STEPS, 4)),
            pltpu.SemaphoreType.DMA((2,)),
            pltpu.SemaphoreType.DMA((4,)),
        ],
        compiler_params=pltpu.CompilerParams(
            collective_id=0, has_side_effects=True, vmem_limit_bytes=48 * 1024 * 1024
        ),
        cost_estimate=pl.CostEstimate(flops=8_000_000, bytes_accessed=800_000, transcendentals=0),
    )(*(
        pltpu.with_memory_space_constraint(given, pltpu.HBM)
        for given in (velocity, density, stored, holders, adjoint, traces, aperture)
    ))
    return pl.pallas_call(
        finish,
        out_shape=tuple(jax.ShapeDtypeStruct(one.shape, f32) for one in results),
        in_specs=[inside] * 3,
        out_specs=(anywhere,) * 3,
        scratch_shapes=[pltpu.SemaphoreType.DMA((3,))],
    )(*(pltpu.with_memory_space_constraint(one, pltpu.VMEM) for one in results))


def solution(mesh):
    return jax.shard_map(
        functools.partial(shards, mesh.shape["gx"], mesh.shape["gy"]),
        mesh=mesh,
        in_specs=(
            P("gx", "gy", "shot"),
            P("gx", "gy", "shot"),
            P("gx", None, ("shot", "gy"), None),
            P("gx", None),
            P("shot", None, "gx", "gy", None),
            P("shot", None, "gx", "gy"),
            P(),
        ),
        out_specs=(
            P("gx", "gy", "shot"),
            P("shot", None, "gx", "gy", None),
            P("shot", None, "gx", "gy", None),
        ),
        check_vma=False,
    )
```

```python
import functools

import jax
import jax.numpy as jnp
from jax import lax
from jax.experimental import pallas as pl
from jax.experimental.pallas import tpu as pltpu
from jax.sharding import PartitionSpec as P

REC_Z = 8
STEPS = 4
LAPLACE_TAPS = (-205.0 / 72.0, 8.0 / 5.0, -1.0 / 5.0, 8.0 / 315.0, -1.0 / 560.0)
SLOPE_TAPS = (4.0 / 5.0, -1.0 / 5.0, 4.0 / 105.0, -1.0 / 280.0)


def y_plus(centre, halo, row, k):
    return pltpu.roll(jnp.where(row < k, halo, centre), 8 - k, 1)


def y_minus(centre, halo, row, k):
    return pltpu.roll(jnp.where(row >= 8 - k, halo, centre), k, 1)


def z_plus(lower, upper, lane, k):
    low, up = pltpu.roll(lower, 128 - k, 2), pltpu.roll(upper, 128 - k, 2)
    return jnp.where(lane < 128 - k, low, up), up


def z_minus(lower, upper, lane, k):
    low, up = pltpu.roll(lower, k, 2), pltpu.roll(upper, k, 2)
    return low, jnp.where(lane >= k, up, low)


def y_plus_outer(centre, above, below, row, k):
    return pltpu.roll(jnp.where(row < k, centre, jnp.where(row < k + 4, above, below)), 8 - k, 1)


def y_minus_outer(centre, above, below, row, k):
    return pltpu.roll(
        jnp.where(row >= 8 - k, centre, jnp.where(row < 4 - k, above, below)), k, 1
    )


def kernel(
    n_x,
    n_y,
    velocity,
    density,
    stored,
    holders,
    adjoint,
    traces,
    aperture,
    image_out,
    forward_out,
    adjoint_out,
    ahead,
    ahead_y,
    wide,
    below,
    above,
    corner,
    ring,
    mid,
    mid_y,
    old,
    back,
    back_y,
    back_old,
    last,
    coef,
    coef_y,
    dens,
    dens_ring,
    dens_far,
    speed,
    speed_y,
    pieces,
    holders_v,
    traces_v,
    aperture_v,
    inject,
    share,
    partner_share,
    small_sem,
    local_sem,
    own_sem,
    piece_sem,
    piece_send,
    model_send,
    model_recv,
    outer_send,
    outer_recv,
    deep_send,
    deep_recv,
    ahead_send,
    ahead_recv,
    back_send,
    back_recv,
    image_sem,
    out_sem,
):
    s, b, j = lax.axis_index("shot"), lax.axis_index("gx"), lax.axis_index("gy")
    other = 1 - s
    f32 = jnp.float32

    smalls = [
        pltpu.make_async_copy(holders, holders_v, small_sem.at[0]),
        pltpu.make_async_copy(traces.at[0], traces_v, small_sem.at[1]),
        pltpu.make_async_copy(aperture, aperture_v, small_sem.at[2]),
    ]
    owns = [
        pltpu.make_async_copy(adjoint.at[0, 0], back.at[0, pl.ds(4, 8)], own_sem.at[0]),
        pltpu.make_async_copy(adjoint.at[0, 1], back_old, own_sem.at[1]),
    ]
    own_model = [
        pltpu.make_async_copy(density, dens.at[s, pl.ds(8, 8)], local_sem.at[0]),
        pltpu.make_async_copy(velocity, speed.at[s, pl.ds(4, 8)], local_sem.at[1]),
        pltpu.make_async_copy(stored.at[b], pieces.at[b], local_sem.at[2]),
    ]

    barrier = pltpu.get_barrier_semaphore()

    def greet(step, carry):
        pl.semaphore_signal(barrier, inc=1, device_id={"gx": lax.rem(b + step, n_x)})
        return carry

    lax.fori_loop(1, n_x, greet, 0)

    def toward(dx, dy, shot=None):
        target = {} if shot is None else {"shot": shot}
        if dx:
            target["gx"] = lax.rem(b + n_x + dx, n_x)
        if dy:
            target["gy"] = lax.rem(j + n_y + dy, n_y)
        return target

    sides = ((1, 0), (-1, 0), (0, 1), (0, -1))
    diagonals = ((1, 1), (1, -1), (-1, 1), (-1, -1))
    near = [{"shot": other}]
    near += [toward(0, dy) for dy in (1, -1)]
    near += [toward(dx, dy) for dx, dy in diagonals]
    near += [toward(dx, dy, other) for dx, dy in sides + diagonals]
    for target in near:
        pl.semaphore_signal(barrier, inc=1, device_id=target)

    for copy in own_model + owns + smalls:
        copy.start()

    def fill(refs, value):
        for ref in refs:
            ref[...] = jnp.full(ref.shape, value, f32)

    @pl.when(b == 0)
    def _():
        fill((wide.at[:8], corner.at[:4], ahead.at[:, :4], back.at[:, :4], speed.at[:, :4]), 0.0)
        fill((dens.at[:, :8], dens_ring.at[:, :4]), 1.0)

    @pl.when(b == n_x - 1)
    def _():
        fill((wide.at[16:], corner.at[4:], ahead.at[:, 12:], back.at[:, 12:], speed.at[:, 12:]), 0.0)
        fill((dens.at[:, 16:], dens_ring.at[:, 12:]), 1.0)

    @pl.when(j == 0)
    def _():
        fill((below, corner.at[:, 4:], ahead_y.at[:, :, 4:], back_y.at[:, :, 4:], speed_y.at[:, :, 4:]), 0.0)
        fill((dens_far.at[:, :, :4], dens_ring.at[:, :, 4:]), 1.0)

    @pl.when(j == n_y - 1)
    def _():
        fill((above, corner.at[:, :4], ahead_y.at[:, :, :4], back_y.at[:, :, :4], speed_y.at[:, :, :4]), 0.0)
        fill((dens_far.at[:, :, 4:], dens_ring.at[:, :, :4]), 1.0)

    pl.semaphore_wait(barrier, n_x - 1 + len(near))

    def send_piece(step, carry):
        target = lax.rem(b + step, n_x)
        pltpu.make_async_remote_copy(
            stored.at[target], pieces.at[b], piece_send, piece_sem, device_id={"gx": target}
        ).start()
        return carry

    lax.fori_loop(1, n_x, send_piece, 0)

    def exists(dx, dy):
        there = b >= 0
        if dx:
            there &= (b < n_x - 1) if dx > 0 else (b > 0)
        if dy:
            there &= (j < n_y - 1) if dy > 0 else (j > 0)
        return there

    class Group:
        def __init__(self, entries, send_sem, recv_sem):
            self.items = []
            for at, (dx, dy, shot, src, dst) in enumerate(entries):
                copy = pltpu.make_async_remote_copy(
                    src, dst, send_sem.at[at], recv_sem.at[at], device_id=toward(dx, dy, shot)
                )
                self.items.append((copy, dx, dy))
            for copy, dx, dy in self.items:
                self.guard(dx, dy, copy.start)

        def guard(self, dx, dy, action):
            if dx or dy:
                pl.when(exists(dx, dy))(action)
            else:
                action()

        def received(self):
            for copy, dx, dy in self.items:
                self.guard(-dx, -dy, copy.wait_recv)

        def sent(self):
            for copy, dx, dy in self.items:
                self.guard(dx, dy, copy.wait_send)

    first, final = pl.ds(0, 4), pl.ds(4, 4)

    def shallow(src, base, planes, rows, shot=None):
        return [
            (1, 0, shot, src.at[pl.ds(base + 4, 4)], planes.at[pl.ds(0, 4)]),
            (-1, 0, shot, src.at[pl.ds(base, 4)], planes.at[pl.ds(12, 4)]),
            (0, 1, shot, src.at[pl.ds(base, 8), final], rows.at[:, final]),
            (0, -1, shot, src.at[pl.ds(base, 8), first], rows.at[:, first]),
        ]

    def deep(src, base, planes, lower, upper, corners, shot=None):
        whole = src.at[pl.ds(base, 8)]
        entries = [
            (1, 0, shot, whole, planes.at[pl.ds(0, 8)]),
            (-1, 0, shot, whole, planes.at[pl.ds(16, 8)]),
        ]
        for dx, dy in diagonals:
            rows = final if dy > 0 else first
            here = pl.ds(base + 4, 4) if dx > 0 else pl.ds(base, 4)
            there = first if dx > 0 else final
            entries.append((dx, dy, shot, src.at[here, rows], corners.at[there, rows]))
        entries.append((0, 1, shot, whole, lower))
        entries.append((0, -1, shot, whole, upper))
        return entries

    backs = [
        Group(
            shallow(adjoint.at[0, 0], 0, back.at[0], back_y.at[0]), back_send.at[0], back_recv.at[0]
        )
    ]

    model = [
        (0, 0, other, density, dens.at[s, pl.ds(8, 8)]),
        (0, 0, other, velocity, speed.at[s, pl.ds(4, 8)]),
    ]
    outer_model = []
    for shot in (s, other):
        ring_s = dens_ring.at[s]
        model += shallow(density, 0, dens.at[s, pl.ds(4, 16)], ring_s.at[pl.ds(4, 8)], shot)
        outer_model += shallow(velocity, 0, speed.at[s], speed_y.at[s], shot)
        outer_model += [
            (1, 0, shot, density.at[first], dens.at[s, pl.ds(0, 4)]),
            (-1, 0, shot, density.at[final], dens.at[s, pl.ds(20, 4)]),
            (0, 1, shot, density.at[:, first], dens_far.at[s, :, first]),
            (0, -1, shot, density.at[:, final], dens_far.at[s, :, final]),
        ]
        for dx, dy in diagonals:
            rows = final if dy > 0 else first
            here, there = (final, first) if dx > 0 else (first, pl.ds(12, 4))
            outer_model.append((dx, dy, shot, density.at[here, rows], ring_s.at[there, rows]))
    model = Group(model, model_send, model_recv)
    groups = [model]

    row = lax.broadcasted_iota(jnp.int32, (1, 8, 128), 1)
    lane = lax.broadcasted_iota(jnp.int32, (1, 8, 128), 2)
    halves = (pl.ds(0, 128), pl.ds(128, 128))

    for copy in smalls:
        copy.wait()
    column = lax.broadcasted_iota(jnp.int32, (64, n_x), 0)
    place = column // 2
    parity = column - 2 * place
    hit = holders_v[...] == place
    picks = [jnp.where(hit & (parity == r), 1.0, 0.0).astype(f32) for r in range(2)]

    bounds = aperture_v[...]
    bounds = jnp.where(s == 0, bounds[0:1], bounds[1:2])
    active = jnp.where((b >= bounds[:, 0:1]) & (b < bounds[:, 1:2]), 1.0, 0.0).astype(f32)
    active = active.reshape(1, 1, 1)

    def coefficients(out, parts, speeds, logs, x_of, plus_of, minus_of):
        def put(at, lanes, value):
            start = 0
            for low, count in parts:
                out[at, low : low + count, :, lanes] = value[start : start + count]
                start += count

        grads = [[0.0, 0.0, 0.0] for half in range(2)]
        for k in range(1, 5):
            tap = SLOPE_TAPS[k - 1]
            ahead = z_plus(logs[0], logs[1], lane, k)
            behind = z_minus(logs[0], logs[1], lane, k)
            ahead = (ahead[0], jnp.where(lane < 128 - k, ahead[1], 0.0))
            behind = (jnp.where(lane >= k, behind[0], 0.0), behind[1])
            for half in range(2):
                grads[half][0] += tap * (x_of(half, k) - x_of(half, -k))
                grads[half][1] += tap * (plus_of(half, k) - minus_of(half, k))
                grads[half][2] += tap * (ahead[half] - behind[half])
        for half, lanes in enumerate(halves):
            sq = speeds(half)
            sq = sq * sq
            put(0, lanes, 2.0 + (3.0 * LAPLACE_TAPS[0]) * sq)
            slopes = [sq * grad for grad in grads[half]]
            for k in range(1, 5):
                even = LAPLACE_TAPS[k] * sq
                for axis in range(3):
                    odd = SLOPE_TAPS[k - 1] * slopes[axis]
                    plus, minus = even - odd, even + odd
                    if axis == 2 and half == 0:
                        minus = jnp.where(lane >= k, minus, 0.0)
                    elif axis == 2:
                        plus = jnp.where(lane < 128 - k, plus, 0.0)
                    at = 1 + 6 * (k - 1) + 2 * axis
                    put(at, lanes, plus)
                    put(at + 1, lanes, minus)

    def steps(count, table, base, centre_of, x_of, plus_of, minus_of, before_of, put):
        def one(p, carry):
            centre = [centre_of(p, lanes) for lanes in halves]
            place = pl.ds(base + p, 1)
            total = [
                table[0, place, :, lanes] * centre[half] - before_of(p, lanes)
                for half, lanes in enumerate(halves)
            ]
            for k in range(1, 5):
                at = 1 + 6 * (k - 1)
                up = z_plus(centre[0], centre[1], lane, k)
                down = z_minus(centre[0], centre[1], lane, k)
                for half, lanes in enumerate(halves):
                    total[half] = (
                        total[half]
                        + table[at, place, :, lanes] * x_of(p, lanes, k)
                        + table[at + 1, place, :, lanes] * x_of(p, lanes, -k)
                        + table[at + 2, place, :, lanes] * plus_of(p, lanes, centre[half], k)
                        + table[at + 3, place, :, lanes] * minus_of(p, lanes, centre[half], k)
                        + table[at + 4, place, :, lanes] * up[half]
                        + table[at + 5, place, :, lanes] * down[half]
                    )
            for half, lanes in enumerate(halves):
                put(p, lanes, total[half], half)
            return carry

        lax.fori_loop(0, count, one, 0, unroll=True)

    def into(ref, base):
        def put(p, lanes, value, half):
            ref[pl.ds(base + p, 1), :, lanes] = value

        return put

    def plane_of(ref, base):
        return lambda p, lanes, k=0: ref[pl.ds(base + p + k, 1), :, lanes]

    def inner_step(planes, rows, before, put, base=4, first_row=0):
        edge = plane_of(rows, first_row)
        steps(
            8,
            coef,
            base,
            plane_of(planes, base),
            plane_of(planes, base),
            lambda p, lanes, centre, k: y_plus(centre, edge(p, lanes), row, k),
            lambda p, lanes, centre, k: y_minus(centre, edge(p, lanes), row, k),
            before,
            put,
        )

    def back_step(level):
        backs[level].received()
        before = plane_of(back_old, 0) if level == 0 else plane_of(back.at[level - 1], 4)
        target = last.at[1] if level == STEPS - 1 else back.at[level + 1]
        start = 0 if level == STEPS - 1 else 4

        def put(p, lanes, value, half):
            if half == 0:
                value = value + inject[STEPS - 1 - level, pl.ds(p, 1)]
            target[pl.ds(start + p, 1), :, lanes] = value

        inner_step(back.at[level], back_y.at[level], before, put)
        if level < STEPS - 1:
            backs.append(
                Group(
                    shallow(back.at[level + 1], 4, back.at[level + 1], back_y.at[level + 1]),
                    back_send.at[level + 1],
                    back_recv.at[level + 1],
                )
            )

    def send_ahead(level):
        group = Group(
            shallow(ahead.at[level], 4, ahead.at[level], ahead_y.at[level]),
            ahead_send.at[level],
            ahead_recv.at[level],
        )
        groups.append(group)
        return group

    own_model[2].wait()
    arrived = pieces.at[pl.ds(0, n_x - 1)]
    pltpu.make_async_copy(arrived, arrived, piece_sem).wait()
    for level in (0, 1):
        found = 0.0
        for r in range(2):
            found += jnp.dot(
                picks[r],
                pieces[:, level, r, :],
                precision=lax.Precision.HIGHEST,
                preferred_element_type=f32,
            )
        found = found.reshape(8, 8, 256)
        if level == 0:
            ahead[0, 4:12] = found
            exchange = send_ahead(0)
        else:
            old[...] = found

    for copy in own_model[:2]:
        copy.wait()
    model.received()
    for half in range(2):
        dens[half, 4:20] = jnp.log(dens[half, 4:20])
        dens_ring[half, 4:12] = jnp.log(dens_ring[half, 4:12])
    coefficients(
        coef,
        ((4, 8),),
        lambda half: speed[half, 4:12],
        [dens[half, 8:16] for half in range(2)],
        lambda half, k: dens[half, 8 + k : 16 + k],
        lambda half, k: y_plus(dens[half, 8:16], dens_ring[half, 4:12], row, k),
        lambda half, k: y_minus(dens[half, 8:16], dens_ring[half, 4:12], row, k),
    )
    eye = lax.broadcasted_iota(jnp.int32, (8, 8), 0) == lax.broadcasted_iota(jnp.int32, (8, 8), 1)
    at_receiver = lax.broadcasted_iota(jnp.int32, (8, 128), 1) == REC_Z
    for x in range(8):
        sq = speed[0, 4 + x] * speed[0, 4 + x]
        for number in range(STEPS):
            line = jnp.where(eye, traces_v[number, pl.ds(x, 1), :], 0.0)
            line = jnp.sum(line, axis=1, keepdims=True)
            inject[number, x] = jnp.where(at_receiver, line, 0.0) * sq

    for copy in owns:
        copy.wait()
    back_step(0)

    outer_model = Group(outer_model, outer_send, outer_recv)
    groups.append(outer_model)

    exchange.received()
    inner_step(ahead.at[0], ahead_y.at[0], plane_of(old, 0), into(ahead.at[1], 4))
    exchange = send_ahead(1)
    back_step(1)
    exchange.received()
    inner_step(ahead.at[1], ahead_y.at[1], plane_of(ahead.at[0], 4), into(wide, 8))
    exchange = Group(deep(wide, 8, wide, below, above, corner), deep_send, deep_recv)
    groups.append(exchange)

    outer_model.received()
    for half in range(2):
        for planes in (slice(0, 4), slice(20, 24)):
            dens[half, planes] = jnp.log(dens[half, planes])
        for planes in (slice(0, 4), slice(12, 16)):
            dens_ring[half, planes] = jnp.log(dens_ring[half, planes])
        dens_far[half] = jnp.log(dens_far[half])

    def both(ref, half, low, high):
        return jnp.concatenate([ref[half, low : low + 4], ref[half, high : high + 4]], axis=0)

    coefficients(
        coef,
        ((0, 4), (12, 4)),
        lambda half: both(speed, half, 0, 12),
        [both(dens, half, 4, 16) for half in range(2)],
        lambda half, k: both(dens, half, 4 + k, 16 + k),
        lambda half, k: y_plus(both(dens, half, 4, 16), both(dens_ring, half, 0, 12), row, k),
        lambda half, k: y_minus(both(dens, half, 4, 16), both(dens_ring, half, 0, 12), row, k),
    )
    dens_above = [
        jnp.where(row < 4, dens_ring[half, 4:12], dens_far[half]) for half in range(2)
    ]
    dens_below = [
        jnp.where(row < 4, dens_far[half], dens_ring[half, 4:12]) for half in range(2)
    ]
    coefficients(
        coef_y,
        ((0, 8),),
        lambda half: speed_y[half],
        [dens_ring[half, 4:12] for half in range(2)],
        lambda half, k: dens_ring[half, 4 + k : 12 + k],
        lambda half, k: y_plus_outer(dens[half, 8:16], dens_above[half], dens_below[half], row, k),
        lambda half, k: y_minus_outer(dens[half, 8:16], dens_above[half], dens_below[half], row, k),
    )

    back_step(2)
    outs = [pltpu.make_async_copy(back.at[3, pl.ds(4, 8)], adjoint_out.at[0, 1], out_sem.at[0])]
    outs[0].start()
    early = [
        ahead[1, 4:12, :, lanes] * back[3, 4:12, :, lanes]
        + wide[8:16, :, lanes] * back[2, 4:12, :, lanes]
        for lanes in halves
    ]

    exchange.received()
    for lanes in halves:
        ring[0:4, :, lanes] = corner[0:4, :, lanes]
        ring[4:12, :, lanes] = jnp.where(row < 4, above[:, :, lanes], below[:, :, lanes])
        ring[12:16, :, lanes] = corner[4:8, :, lanes]
    low, mine, up = plane_of(below, 0), plane_of(wide, 8), plane_of(above, 0)
    steps(
        8,
        coef_y,
        0,
        plane_of(ring, 4),
        plane_of(ring, 4),
        lambda p, lanes, centre, k: y_plus_outer(
            mine(p, lanes), up(p, lanes), low(p, lanes), row, k
        ),
        lambda p, lanes, centre, k: y_minus_outer(
            mine(p, lanes), up(p, lanes), low(p, lanes), row, k
        ),
        plane_of(ahead_y.at[1], 0),
        into(mid_y, 0),
    )
    around = plane_of(ring, 0)
    steps(
        16,
        coef,
        0,
        plane_of(wide, 4),
        plane_of(wide, 4),
        lambda p, lanes, centre, k: y_plus(centre, around(p, lanes), row, k),
        lambda p, lanes, centre, k: y_minus(centre, around(p, lanes), row, k),
        plane_of(ahead.at[1], 0),
        into(mid, 0),
    )
    outs.append(pltpu.make_async_copy(mid.at[pl.ds(4, 8)], forward_out.at[0, 1], out_sem.at[1]))
    outs[1].start()
    inner_step(mid, mid_y, plane_of(wide, 8), into(last.at[0], 0))
    whole = [
        active
        * (
            early[half]
            + mid[4:12, :, lanes] * back[1, 4:12, :, lanes]
            + last[0, :, :, lanes] * back[0, 4:12, :, lanes]
        )
        for half, lanes in enumerate(halves)
    ]
    share[...] = jnp.where(s == 0, whole[1], whole[0])
    to_partner = pltpu.make_async_remote_copy(
        share, partner_share, image_sem.at[0], image_sem.at[1], device_id={"shot": other}
    )
    to_partner.start()
    outs.append(pltpu.make_async_copy(last.at[0], forward_out.at[0, 0], out_sem.at[2]))
    outs[2].start()
    image_out[...] = jnp.where(s == 0, whole[0], whole[1])

    back_step(3)
    outs.append(pltpu.make_async_copy(last.at[1], adjoint_out.at[0, 0], out_sem.at[3]))
    outs[3].start()

    gone = stored.at[pl.ds(0, n_x - 1)]
    pltpu.make_async_copy(gone, gone, piece_send).wait()
    for group in groups + backs:
        group.sent()

    to_partner.wait()
    image_out[...] += partner_share[...]
    for copy in outs:
        copy.wait()


def finish(image, forward, adjoint, image_out, forward_out, adjoint_out, sem):
    copies = [
        pltpu.make_async_copy(src, dst, sem.at[at])
        for at, (src, dst) in enumerate(
            ((image, image_out), (forward, forward_out), (adjoint, adjoint_out))
        )
    ]
    for copy in copies:
        copy.start()
    for copy in copies:
        copy.wait()


def shards(n_x, n_y, velocity, density, stored, holders, adjoint, traces, aperture):
    f32 = jnp.float32
    anywhere = pl.BlockSpec(memory_space=pl.ANY)
    inside = pl.BlockSpec(memory_space=pltpu.VMEM)
    results = pl.pallas_call(
        functools.partial(kernel, n_x, n_y),
        out_shape=(
            pltpu.VMEM((8, 8, 128), f32),
            pltpu.VMEM((1, 2, 8, 8, 256), f32),
            pltpu.VMEM((1, 2, 8, 8, 256), f32),
        ),
        in_specs=[anywhere] * 7,
        out_specs=(inside,) * 3,
        scratch_shapes=[
            pltpu.VMEM((2, 16, 8, 256), f32),
            pltpu.VMEM((2, 8, 8, 256), f32),
            pltpu.VMEM((24, 8, 256), f32),
            pltpu.VMEM((8, 8, 256), f32),
            pltpu.VMEM((8, 8, 256), f32),
            pltpu.VMEM((8, 8, 256), f32),
            pltpu.VMEM((16, 8, 256), f32),
            pltpu.VMEM((16, 8, 256), f32),
            pltpu.VMEM((8, 8, 256), f32),
            pltpu.VMEM((8, 8, 256), f32),
            pltpu.VMEM((STEPS, 16, 8, 256), f32),
            pltpu.VMEM((STEPS, 8, 8, 256), f32),
            pltpu.VMEM((8, 8, 256), f32),
            pltpu.VMEM((2, 8, 8, 256), f32),
            pltpu.VMEM((25, 16, 8, 256), f32),
            pltpu.VMEM((25, 8, 8, 256), f32),
            pltpu.VMEM((2, 24, 8, 128), f32),
            pltpu.VMEM((2, 16, 8, 128), f32),
            pltpu.VMEM((2, 8, 8, 128), f32),
            pltpu.VMEM((2, 16, 8, 128), f32),
            pltpu.VMEM((2, 8, 8, 128), f32),
            pltpu.VMEM((n_x, 2, 2, 256), f32),
            pltpu.VMEM((1, n_x), jnp.int32),
            pltpu.VMEM((STEPS, 8, 8), f32),
            pltpu.VMEM((2, 2), jnp.int32),
            pltpu.VMEM((STEPS, 8, 8, 128), f32),
            pltpu.VMEM((8, 8, 128), f32),
            pltpu.VMEM((8, 8, 128), f32),
            pltpu.SemaphoreType.DMA((3,)),
            pltpu.SemaphoreType.DMA((3,)),
            pltpu.SemaphoreType.DMA((2,)),
            pltpu.SemaphoreType.DMA,
            pltpu.SemaphoreType.DMA,
            pltpu.SemaphoreType.DMA((10,)),
            pltpu.SemaphoreType.DMA((10,)),
            pltpu.SemaphoreType.DMA((24,)),
            pltpu.SemaphoreType.DMA((24,)),
            pltpu.SemaphoreType.DMA((8,)),
            pltpu.SemaphoreType.DMA((8,)),
            pltpu.SemaphoreType.DMA((2, 4)),
            pltpu.SemaphoreType.DMA((2, 4)),
            pltpu.SemaphoreType.DMA((STEPS, 4)),
            pltpu.SemaphoreType.DMA((STEPS, 4)),
            pltpu.SemaphoreType.DMA((2,)),
            pltpu.SemaphoreType.DMA((4,)),
        ],
        compiler_params=pltpu.CompilerParams(
            collective_id=0, has_side_effects=True, vmem_limit_bytes=48 * 1024 * 1024
        ),
        cost_estimate=pl.CostEstimate(flops=8_000_000, bytes_accessed=800_000, transcendentals=0),
    )(*(
        pltpu.with_memory_space_constraint(given, pltpu.HBM)
        for given in (velocity, density, stored, holders, adjoint, traces, aperture)
    ))
    return pl.pallas_call(
        finish,
        out_shape=tuple(jax.ShapeDtypeStruct(one.shape, f32) for one in results),
        in_specs=[inside] * 3,
        out_specs=(anywhere,) * 3,
        scratch_shapes=[pltpu.SemaphoreType.DMA((3,))],
    )(*(pltpu.with_memory_space_constraint(one, pltpu.VMEM) for one in results))


def solution(mesh):
    return jax.shard_map(
        functools.partial(shards, mesh.shape["gx"], mesh.shape["gy"]),
        mesh=mesh,
        in_specs=(
            P("gx", "gy", "shot"),
            P("gx", "gy", "shot"),
            P("gx", None, ("shot", "gy"), None),
            P("gx", None),
            P("shot", None, "gx", "gy", None),
            P("shot", None, "gx", "gy"),
            P(),
        ),
        out_specs=(
            P("gx", "gy", "shot"),
            P("shot", None, "gx", "gy", None),
            P("shot", None, "gx", "gy", None),
        ),
        check_vma=False,
    )
```

```python
import functools

import jax
import jax.numpy as jnp
from jax import lax
from jax.experimental import pallas as pl
from jax.experimental.pallas import tpu as pltpu
from jax.sharding import PartitionSpec as P

REC_Z = 8
STEPS = 4
LAPLACE_TAPS = (-205.0 / 72.0, 8.0 / 5.0, -1.0 / 5.0, 8.0 / 315.0, -1.0 / 560.0)
SLOPE_TAPS = (4.0 / 5.0, -1.0 / 5.0, 4.0 / 105.0, -1.0 / 280.0)


def y_plus(centre, halo, row, k):
    return pltpu.roll(jnp.where(row < k, halo, centre), 8 - k, 1)


def y_minus(centre, halo, row, k):
    return pltpu.roll(jnp.where(row >= 8 - k, halo, centre), k, 1)


def z_plus(lower, upper, lane, k):
    low, up = pltpu.roll(lower, 128 - k, 2), pltpu.roll(upper, 128 - k, 2)
    return jnp.where(lane < 128 - k, low, up), up


def z_minus(lower, upper, lane, k):
    low, up = pltpu.roll(lower, k, 2), pltpu.roll(upper, k, 2)
    return low, jnp.where(lane >= k, up, low)


def y_plus_outer(centre, above, below, row, k):
    return pltpu.roll(jnp.where(row < k, centre, jnp.where(row < k + 4, above, below)), 8 - k, 1)


def y_minus_outer(centre, above, below, row, k):
    return pltpu.roll(
        jnp.where(row >= 8 - k, centre, jnp.where(row < 4 - k, above, below)), k, 1
    )


def kernel(
    n_x,
    n_y,
    velocity,
    density,
    stored,
    holders,
    adjoint,
    traces,
    aperture,
    image_out,
    forward_out,
    adjoint_out,
    ahead,
    ahead_y,
    wide,
    below,
    above,
    corner,
    ring,
    mid,
    mid_y,
    old,
    back,
    back_y,
    back_old,
    last,
    coef,
    coef_y,
    dens,
    dens_ring,
    dens_far,
    speed,
    speed_y,
    pieces,
    holders_v,
    traces_v,
    aperture_v,
    inject,
    share,
    partner_share,
    small_sem,
    local_sem,
    own_sem,
    piece_sem,
    piece_send,
    model_send,
    model_recv,
    outer_send,
    outer_recv,
    hand_send,
    hand_recv,
    deep_send,
    deep_recv,
    ahead_send,
    ahead_recv,
    back_send,
    back_recv,
    image_sem,
    out_sem,
):
    s, b, j = lax.axis_index("shot"), lax.axis_index("gx"), lax.axis_index("gy")
    other = 1 - s
    f32 = jnp.float32

    smalls = [
        pltpu.make_async_copy(holders, holders_v, small_sem.at[0]),
        pltpu.make_async_copy(traces.at[0], traces_v, small_sem.at[1]),
        pltpu.make_async_copy(aperture, aperture_v, small_sem.at[2]),
    ]
    owns = [
        pltpu.make_async_copy(adjoint.at[0, 0], back.at[0, pl.ds(4, 8)], own_sem.at[0]),
        pltpu.make_async_copy(adjoint.at[0, 1], back_old, own_sem.at[1]),
    ]
    own_model = [
        pltpu.make_async_copy(density, dens.at[s, pl.ds(8, 8)], local_sem.at[0]),
        pltpu.make_async_copy(velocity, speed.at[s, pl.ds(4, 8)], local_sem.at[1]),
        pltpu.make_async_copy(stored.at[b], pieces.at[b], local_sem.at[2]),
    ]

    barrier = pltpu.get_barrier_semaphore()

    def greet(step, carry):
        pl.semaphore_signal(barrier, inc=1, device_id={"gx": lax.rem(b + step, n_x)})
        return carry

    lax.fori_loop(1, n_x, greet, 0)

    def toward(dx, dy, shot=None):
        target = {} if shot is None else {"shot": shot}
        if dx:
            target["gx"] = lax.rem(b + n_x + dx, n_x)
        if dy:
            target["gy"] = lax.rem(j + n_y + dy, n_y)
        return target

    sides = ((1, 0), (-1, 0), (0, 1), (0, -1))
    diagonals = ((1, 1), (1, -1), (-1, 1), (-1, -1))
    near = [{"shot": other}]
    near += [toward(0, dy) for dy in (1, -1)]
    near += [toward(dx, dy) for dx, dy in diagonals]
    near += [toward(dx, dy, other) for dx, dy in sides]
    for target in near:
        pl.semaphore_signal(barrier, inc=1, device_id=target)

    for copy in own_model + owns + smalls:
        copy.start()

    def fill(refs, value):
        for ref in refs:
            ref[...] = jnp.full(ref.shape, value, f32)

    low4, high4 = pl.ds(0, 4), pl.ds(4, 4)

    @pl.when(b == 0)
    def _():
        fill((wide.at[:8], corner.at[:4], ahead.at[:, :4], back.at[:, :4], speed.at[s, low4]), 0.0)
        fill((dens.at[:, 4:8],), 1.0)
        fill((dens.at[s, low4], dens_ring.at[s, low4]), 1.0)

    @pl.when(b == n_x - 1)
    def _():
        fill((wide.at[16:], corner.at[4:], ahead.at[:, 12:], back.at[:, 12:]), 0.0)
        fill((speed.at[s, pl.ds(12, 4)],), 0.0)
        fill((dens.at[:, 16:20],), 1.0)
        fill((dens.at[s, pl.ds(20, 4)], dens_ring.at[s, pl.ds(12, 4)]), 1.0)

    @pl.when(j == 0)
    def _():
        fill((below, corner.at[:, 4:], ahead_y.at[:, :, 4:], back_y.at[:, :, 4:]), 0.0)
        fill((speed_y.at[s, :, high4],), 0.0)
        fill((dens_ring.at[:, 4:12, 4:],), 1.0)
        fill((dens_far.at[s, :, low4], dens_ring.at[s, :, high4]), 1.0)

    @pl.when(j == n_y - 1)
    def _():
        fill((above, corner.at[:, :4], ahead_y.at[:, :, :4], back_y.at[:, :, :4]), 0.0)
        fill((speed_y.at[s, :, low4],), 0.0)
        fill((dens_ring.at[:, 4:12, :4],), 1.0)
        fill((dens_far.at[s, :, high4], dens_ring.at[s, :, low4]), 1.0)

    pl.semaphore_wait(barrier, n_x - 1 + len(near))

    def send_piece(step, carry):
        target = lax.rem(b + step, n_x)
        pltpu.make_async_remote_copy(
            stored.at[target], pieces.at[b], piece_send, piece_sem, device_id={"gx": target}
        ).start()
        return carry

    lax.fori_loop(1, n_x, send_piece, 0)

    def exists(dx, dy):
        there = b >= 0
        if dx:
            there &= (b < n_x - 1) if dx > 0 else (b > 0)
        if dy:
            there &= (j < n_y - 1) if dy > 0 else (j > 0)
        return there

    class Group:
        def __init__(self, entries, send_sem, recv_sem):
            self.items = []
            for at, (dx, dy, shot, src, dst) in enumerate(entries):
                copy = pltpu.make_async_remote_copy(
                    src, dst, send_sem.at[at], recv_sem.at[at], device_id=toward(dx, dy, shot)
                )
                self.items.append((copy, dx, dy))
            for copy, dx, dy in self.items:
                self.guard(dx, dy, copy.start)

        def guard(self, dx, dy, action):
            if dx or dy:
                pl.when(exists(dx, dy))(action)
            else:
                action()

        def received(self):
            for copy, dx, dy in self.items:
                self.guard(-dx, -dy, copy.wait_recv)

        def sent(self):
            for copy, dx, dy in self.items:
                self.guard(dx, dy, copy.wait_send)

    first, final = pl.ds(0, 4), pl.ds(4, 4)

    def shallow(src, base, planes, rows, shot=None):
        return [
            (1, 0, shot, src.at[pl.ds(base + 4, 4)], planes.at[pl.ds(0, 4)]),
            (-1, 0, shot, src.at[pl.ds(base, 4)], planes.at[pl.ds(12, 4)]),
            (0, 1, shot, src.at[pl.ds(base, 8), final], rows.at[:, final]),
            (0, -1, shot, src.at[pl.ds(base, 8), first], rows.at[:, first]),
        ]

    def deep(src, base, planes, lower, upper, corners, shot=None):
        whole = src.at[pl.ds(base, 8)]
        entries = [
            (1, 0, shot, whole, planes.at[pl.ds(0, 8)]),
            (-1, 0, shot, whole, planes.at[pl.ds(16, 8)]),
        ]
        for dx, dy in diagonals:
            rows = final if dy > 0 else first
            here = pl.ds(base + 4, 4) if dx > 0 else pl.ds(base, 4)
            there = first if dx > 0 else final
            entries.append((dx, dy, shot, src.at[here, rows], corners.at[there, rows]))
        entries.append((0, 1, shot, whole, lower))
        entries.append((0, -1, shot, whole, upper))
        return entries

    backs = [
        Group(
            shallow(adjoint.at[0, 0], 0, back.at[0], back_y.at[0]), back_send.at[0], back_recv.at[0]
        )
    ]

    ring_s = dens_ring.at[s]
    model = [
        (0, 0, other, density, dens.at[s, pl.ds(8, 8)]),
        (0, 0, other, velocity, speed.at[s, pl.ds(4, 8)]),
    ]
    for shot in (None, other):
        model += shallow(density, 0, dens.at[s, pl.ds(4, 16)], ring_s.at[pl.ds(4, 8)], shot)
    model = Group(model, model_send, model_recv)
    outer_model = shallow(velocity, 0, speed.at[s], speed_y.at[s])
    outer_model += [
        (1, 0, None, density.at[first], dens.at[s, pl.ds(0, 4)]),
        (-1, 0, None, density.at[final], dens.at[s, pl.ds(20, 4)]),
        (0, 1, None, density.at[:, first], dens_far.at[s, :, first]),
        (0, -1, None, density.at[:, final], dens_far.at[s, :, final]),
    ]
    for dx, dy in diagonals:
        rows = final if dy > 0 else first
        here, there = (final, first) if dx > 0 else (first, pl.ds(12, 4))
        outer_model.append((dx, dy, None, density.at[here, rows], ring_s.at[there, rows]))
    groups = [model]

    row = lax.broadcasted_iota(jnp.int32, (1, 8, 128), 1)
    lane = lax.broadcasted_iota(jnp.int32, (1, 8, 128), 2)
    halves = (pl.ds(0, 128), pl.ds(128, 128))

    for copy in smalls:
        copy.wait()
    column = lax.broadcasted_iota(jnp.int32, (64, n_x), 0)
    place = column // 2
    parity = column - 2 * place
    hit = holders_v[...] == place
    picks = [jnp.where(hit & (parity == r), 1.0, 0.0).astype(f32) for r in range(2)]

    bounds = aperture_v[...]
    bounds = jnp.where(s == 0, bounds[0:1], bounds[1:2])
    active = jnp.where((b >= bounds[:, 0:1]) & (b < bounds[:, 1:2]), 1.0, 0.0).astype(f32)
    active = active.reshape(1, 1, 1)

    def coefficients(out, parts, speeds, logs, x_of, plus_of, minus_of):
        def put(at, lanes, value):
            start = 0
            for low, count in parts:
                out[at, low : low + count, :, lanes] = value[start : start + count]
                start += count

        grads = [[0.0, 0.0, 0.0] for half in range(2)]
        for k in range(1, 5):
            tap = SLOPE_TAPS[k - 1]
            ahead = z_plus(logs[0], logs[1], lane, k)
            behind = z_minus(logs[0], logs[1], lane, k)
            ahead = (ahead[0], jnp.where(lane < 128 - k, ahead[1], 0.0))
            behind = (jnp.where(lane >= k, behind[0], 0.0), behind[1])
            for half in range(2):
                grads[half][0] += tap * (x_of(half, k) - x_of(half, -k))
                grads[half][1] += tap * (plus_of(half, k) - minus_of(half, k))
                grads[half][2] += tap * (ahead[half] - behind[half])
        for half, lanes in enumerate(halves):
            sq = speeds(half)
            sq = sq * sq
            put(0, lanes, 2.0 + (3.0 * LAPLACE_TAPS[0]) * sq)
            slopes = [sq * grad for grad in grads[half]]
            for k in range(1, 5):
                even = LAPLACE_TAPS[k] * sq
                for axis in range(3):
                    odd = SLOPE_TAPS[k - 1] * slopes[axis]
                    plus, minus = even - odd, even + odd
                    if axis == 2 and half == 0:
                        minus = jnp.where(lane >= k, minus, 0.0)
                    elif axis == 2:
                        plus = jnp.where(lane < 128 - k, plus, 0.0)
                    at = 1 + 6 * (k - 1) + 2 * axis
                    put(at, lanes, plus)
                    put(at + 1, lanes, minus)

    def steps(count, table, base, centre_of, x_of, plus_of, minus_of, before_of, put):
        def one(p, carry):
            centre = [centre_of(p, lanes) for lanes in halves]
            place = pl.ds(base + p, 1)
            total = [
                table[0, place, :, lanes] * centre[half] - before_of(p, lanes)
                for half, lanes in enumerate(halves)
            ]
            for k in range(1, 5):
                at = 1 + 6 * (k - 1)
                up = z_plus(centre[0], centre[1], lane, k)
                down = z_minus(centre[0], centre[1], lane, k)
                for half, lanes in enumerate(halves):
                    total[half] = (
                        total[half]
                        + table[at, place, :, lanes] * x_of(p, lanes, k)
                        + table[at + 1, place, :, lanes] * x_of(p, lanes, -k)
                        + table[at + 2, place, :, lanes] * plus_of(p, lanes, centre[half], k)
                        + table[at + 3, place, :, lanes] * minus_of(p, lanes, centre[half], k)
                        + table[at + 4, place, :, lanes] * up[half]
                        + table[at + 5, place, :, lanes] * down[half]
                    )
            for half, lanes in enumerate(halves):
                put(p, lanes, total[half], half)
            return carry

        lax.fori_loop(0, count, one, 0, unroll=True)

    def into(ref, base):
        def put(p, lanes, value, half):
            ref[pl.ds(base + p, 1), :, lanes] = value

        return put

    def plane_of(ref, base):
        return lambda p, lanes, k=0: ref[pl.ds(base + p + k, 1), :, lanes]

    def inner_step(planes, rows, before, put, base=4, first_row=0):
        edge = plane_of(rows, first_row)
        steps(
            8,
            coef,
            base,
            plane_of(planes, base),
            plane_of(planes, base),
            lambda p, lanes, centre, k: y_plus(centre, edge(p, lanes), row, k),
            lambda p, lanes, centre, k: y_minus(centre, edge(p, lanes), row, k),
            before,
            put,
        )

    def back_step(level):
        backs[level].received()
        before = plane_of(back_old, 0) if level == 0 else plane_of(back.at[level - 1], 4)
        target = last.at[1] if level == STEPS - 1 else back.at[level + 1]
        start = 0 if level == STEPS - 1 else 4

        def put(p, lanes, value, half):
            if half == 0:
                value = value + inject[STEPS - 1 - level, pl.ds(p, 1)]
            target[pl.ds(start + p, 1), :, lanes] = value

        inner_step(back.at[level], back_y.at[level], before, put)
        if level < STEPS - 1:
            backs.append(
                Group(
                    shallow(back.at[level + 1], 4, back.at[level + 1], back_y.at[level + 1]),
                    back_send.at[level + 1],
                    back_recv.at[level + 1],
                )
            )

    def send_ahead(level):
        group = Group(
            shallow(ahead.at[level], 4, ahead.at[level], ahead_y.at[level]),
            ahead_send.at[level],
            ahead_recv.at[level],
        )
        groups.append(group)
        return group

    outer_model = Group(outer_model, outer_send, outer_recv)
    groups.append(outer_model)

    own_model[2].wait()
    arrived = pieces.at[pl.ds(0, n_x - 1)]
    pltpu.make_async_copy(arrived, arrived, piece_sem).wait()
    for level in (0, 1):
        found = 0.0
        for r in range(2):
            found += jnp.dot(
                picks[r],
                pieces[:, level, r, :],
                precision=lax.Precision.HIGHEST,
                preferred_element_type=f32,
            )
        found = found.reshape(8, 8, 256)
        if level == 0:
            ahead[0, 4:12] = found
            exchange = send_ahead(0)
        else:
            old[...] = found

    for copy in own_model[:2]:
        copy.wait()
    model.received()
    for half in range(2):
        dens[half, 4:20] = jnp.log(dens[half, 4:20])
        dens_ring[half, 4:12] = jnp.log(dens_ring[half, 4:12])
    coefficients(
        coef,
        ((4, 8),),
        lambda half: speed[half, 4:12],
        [dens[half, 8:16] for half in range(2)],
        lambda half, k: dens[half, 8 + k : 16 + k],
        lambda half, k: y_plus(dens[half, 8:16], dens_ring[half, 4:12], row, k),
        lambda half, k: y_minus(dens[half, 8:16], dens_ring[half, 4:12], row, k),
    )
    eye = lax.broadcasted_iota(jnp.int32, (8, 8), 0) == lax.broadcasted_iota(jnp.int32, (8, 8), 1)
    at_receiver = lax.broadcasted_iota(jnp.int32, (8, 128), 1) == REC_Z
    for x in range(8):
        sq = speed[0, 4 + x] * speed[0, 4 + x]
        for number in range(STEPS):
            line = jnp.where(eye, traces_v[number, pl.ds(x, 1), :], 0.0)
            line = jnp.sum(line, axis=1, keepdims=True)
            inject[number, x] = jnp.where(at_receiver, line, 0.0) * sq

    for copy in owns:
        copy.wait()
    back_step(0)

    exchange.received()
    inner_step(ahead.at[0], ahead_y.at[0], plane_of(old, 0), into(ahead.at[1], 4))
    exchange = send_ahead(1)
    outer_model.received()
    for planes in (pl.ds(0, 4), pl.ds(20, 4)):
        dens[s, planes] = jnp.log(dens[s, planes])
    for planes in (pl.ds(0, 4), pl.ds(12, 4)):
        dens_ring[s, planes] = jnp.log(dens_ring[s, planes])
    dens_far[s] = jnp.log(dens_far[s])
    handed = [
        ref.at[s, pl.ds(start, count)]
        for ref, start, count in (
            (speed, 0, 4),
            (speed, 12, 4),
            (speed_y, 0, 8),
            (dens, 0, 4),
            (dens, 20, 4),
            (dens_ring, 0, 4),
            (dens_ring, 12, 4),
            (dens_far, 0, 8),
        )
    ]
    handed = Group([(0, 0, other, ref, ref) for ref in handed], hand_send, hand_recv)
    groups.append(handed)
    back_step(1)
    exchange.received()
    inner_step(ahead.at[1], ahead_y.at[1], plane_of(ahead.at[0], 4), into(wide, 8))
    exchange = Group(deep(wide, 8, wide, below, above, corner), deep_send, deep_recv)
    groups.append(exchange)

    handed.received()

    def both(ref, half, low, high):
        return jnp.concatenate([ref[half, low : low + 4], ref[half, high : high + 4]], axis=0)

    coefficients(
        coef,
        ((0, 4), (12, 4)),
        lambda half: both(speed, half, 0, 12),
        [both(dens, half, 4, 16) for half in range(2)],
        lambda half, k: both(dens, half, 4 + k, 16 + k),
        lambda half, k: y_plus(both(dens, half, 4, 16), both(dens_ring, half, 0, 12), row, k),
        lambda half, k: y_minus(both(dens, half, 4, 16), both(dens_ring, half, 0, 12), row, k),
    )
    dens_above = [
        jnp.where(row < 4, dens_ring[half, 4:12], dens_far[half]) for half in range(2)
    ]
    dens_below = [
        jnp.where(row < 4, dens_far[half], dens_ring[half, 4:12]) for half in range(2)
    ]
    coefficients(
        coef_y,
        ((0, 8),),
        lambda half: speed_y[half],
        [dens_ring[half, 4:12] for half in range(2)],
        lambda half, k: dens_ring[half, 4 + k : 12 + k],
        lambda half, k: y_plus_outer(dens[half, 8:16], dens_above[half], dens_below[half], row, k),
        lambda half, k: y_minus_outer(dens[half, 8:16], dens_above[half], dens_below[half], row, k),
    )

    back_step(2)
    outs = [pltpu.make_async_copy(back.at[3, pl.ds(4, 8)], adjoint_out.at[0, 1], out_sem.at[0])]
    outs[0].start()
    early = [
        ahead[1, 4:12, :, lanes] * back[3, 4:12, :, lanes]
        + wide[8:16, :, lanes] * back[2, 4:12, :, lanes]
        for lanes in halves
    ]

    exchange.received()
    for lanes in halves:
        ring[0:4, :, lanes] = corner[0:4, :, lanes]
        ring[4:12, :, lanes] = jnp.where(row < 4, above[:, :, lanes], below[:, :, lanes])
        ring[12:16, :, lanes] = corner[4:8, :, lanes]
    low, mine, up = plane_of(below, 0), plane_of(wide, 8), plane_of(above, 0)
    steps(
        8,
        coef_y,
        0,
        plane_of(ring, 4),
        plane_of(ring, 4),
        lambda p, lanes, centre, k: y_plus_outer(
            mine(p, lanes), up(p, lanes), low(p, lanes), row, k
        ),
        lambda p, lanes, centre, k: y_minus_outer(
            mine(p, lanes), up(p, lanes), low(p, lanes), row, k
        ),
        plane_of(ahead_y.at[1], 0),
        into(mid_y, 0),
    )
    around = plane_of(ring, 0)
    steps(
        16,
        coef,
        0,
        plane_of(wide, 4),
        plane_of(wide, 4),
        lambda p, lanes, centre, k: y_plus(centre, around(p, lanes), row, k),
        lambda p, lanes, centre, k: y_minus(centre, around(p, lanes), row, k),
        plane_of(ahead.at[1], 0),
        into(mid, 0),
    )
    outs.append(pltpu.make_async_copy(mid.at[pl.ds(4, 8)], forward_out.at[0, 1], out_sem.at[1]))
    outs[1].start()
    inner_step(mid, mid_y, plane_of(wide, 8), into(last.at[0], 0))
    whole = [
        active
        * (
            early[half]
            + mid[4:12, :, lanes] * back[1, 4:12, :, lanes]
            + last[0, :, :, lanes] * back[0, 4:12, :, lanes]
        )
        for half, lanes in enumerate(halves)
    ]
    share[...] = jnp.where(s == 0, whole[1], whole[0])
    to_partner = pltpu.make_async_remote_copy(
        share, partner_share, image_sem.at[0], image_sem.at[1], device_id={"shot": other}
    )
    to_partner.start()
    outs.append(pltpu.make_async_copy(last.at[0], forward_out.at[0, 0], out_sem.at[2]))
    outs[2].start()
    image_out[...] = jnp.where(s == 0, whole[0], whole[1])

    back_step(3)
    outs.append(pltpu.make_async_copy(last.at[1], adjoint_out.at[0, 0], out_sem.at[3]))
    outs[3].start()

    gone = stored.at[pl.ds(0, n_x - 1)]
    pltpu.make_async_copy(gone, gone, piece_send).wait()
    for group in groups + backs:
        group.sent()

    to_partner.wait()
    image_out[...] += partner_share[...]
    for copy in outs:
        copy.wait()


def finish(image, forward, adjoint, image_out, forward_out, adjoint_out, sem):
    copies = [
        pltpu.make_async_copy(src, dst, sem.at[at])
        for at, (src, dst) in enumerate(
            ((image, image_out), (forward, forward_out), (adjoint, adjoint_out))
        )
    ]
    for copy in copies:
        copy.start()
    for copy in copies:
        copy.wait()


def shards(n_x, n_y, velocity, density, stored, holders, adjoint, traces, aperture):
    f32 = jnp.float32
    anywhere = pl.BlockSpec(memory_space=pl.ANY)
    inside = pl.BlockSpec(memory_space=pltpu.VMEM)
    results = pl.pallas_call(
        functools.partial(kernel, n_x, n_y),
        out_shape=(
            pltpu.VMEM((8, 8, 128), f32),
            pltpu.VMEM((1, 2, 8, 8, 256), f32),
            pltpu.VMEM((1, 2, 8, 8, 256), f32),
        ),
        in_specs=[anywhere] * 7,
        out_specs=(inside,) * 3,
        scratch_shapes=[
            pltpu.VMEM((2, 16, 8, 256), f32),
            pltpu.VMEM((2, 8, 8, 256), f32),
            pltpu.VMEM((24, 8, 256), f32),
            pltpu.VMEM((8, 8, 256), f32),
            pltpu.VMEM((8, 8, 256), f32),
            pltpu.VMEM((8, 8, 256), f32),
            pltpu.VMEM((16, 8, 256), f32),
            pltpu.VMEM((16, 8, 256), f32),
            pltpu.VMEM((8, 8, 256), f32),
            pltpu.VMEM((8, 8, 256), f32),
            pltpu.VMEM((STEPS, 16, 8, 256), f32),
            pltpu.VMEM((STEPS, 8, 8, 256), f32),
            pltpu.VMEM((8, 8, 256), f32),
            pltpu.VMEM((2, 8, 8, 256), f32),
            pltpu.VMEM((25, 16, 8, 256), f32),
            pltpu.VMEM((25, 8, 8, 256), f32),
            pltpu.VMEM((2, 24, 8, 128), f32),
            pltpu.VMEM((2, 16, 8, 128), f32),
            pltpu.VMEM((2, 8, 8, 128), f32),
            pltpu.VMEM((2, 16, 8, 128), f32),
            pltpu.VMEM((2, 8, 8, 128), f32),
            pltpu.VMEM((n_x, 2, 2, 256), f32),
            pltpu.VMEM((1, n_x), jnp.int32),
            pltpu.VMEM((STEPS, 8, 8), f32),
            pltpu.VMEM((2, 2), jnp.int32),
            pltpu.VMEM((STEPS, 8, 8, 128), f32),
            pltpu.VMEM((8, 8, 128), f32),
            pltpu.VMEM((8, 8, 128), f32),
            pltpu.SemaphoreType.DMA((3,)),
            pltpu.SemaphoreType.DMA((3,)),
            pltpu.SemaphoreType.DMA((2,)),
            pltpu.SemaphoreType.DMA,
            pltpu.SemaphoreType.DMA,
            pltpu.SemaphoreType.DMA((10,)),
            pltpu.SemaphoreType.DMA((10,)),
            pltpu.SemaphoreType.DMA((12,)),
            pltpu.SemaphoreType.DMA((12,)),
            pltpu.SemaphoreType.DMA((8,)),
            pltpu.SemaphoreType.DMA((8,)),
            pltpu.SemaphoreType.DMA((8,)),
            pltpu.SemaphoreType.DMA((8,)),
            pltpu.SemaphoreType.DMA((2, 4)),
            pltpu.SemaphoreType.DMA((2, 4)),
            pltpu.SemaphoreType.DMA((STEPS, 4)),
            pltpu.SemaphoreType.DMA((STEPS, 4)),
            pltpu.SemaphoreType.DMA((2,)),
            pltpu.SemaphoreType.DMA((4,)),
        ],
        compiler_params=pltpu.CompilerParams(
            collective_id=0, has_side_effects=True, vmem_limit_bytes=48 * 1024 * 1024
        ),
        cost_estimate=pl.CostEstimate(flops=8_000_000, bytes_accessed=800_000, transcendentals=0),
    )(*(
        pltpu.with_memory_space_constraint(given, pltpu.HBM)
        for given in (velocity, density, stored, holders, adjoint, traces, aperture)
    ))
    return pl.pallas_call(
        finish,
        out_shape=tuple(jax.ShapeDtypeStruct(one.shape, f32) for one in results),
        in_specs=[inside] * 3,
        out_specs=(anywhere,) * 3,
        scratch_shapes=[pltpu.SemaphoreType.DMA((3,))],
    )(*(pltpu.with_memory_space_constraint(one, pltpu.VMEM) for one in results))


def solution(mesh):
    return jax.shard_map(
        functools.partial(shards, mesh.shape["gx"], mesh.shape["gy"]),
        mesh=mesh,
        in_specs=(
            P("gx", "gy", "shot"),
            P("gx", "gy", "shot"),
            P("gx", None, ("shot", "gy"), None),
            P("gx", None),
            P("shot", None, "gx", "gy", None),
            P("shot", None, "gx", "gy"),
            P(),
        ),
        out_specs=(
            P("gx", "gy", "shot"),
            P("shot", None, "gx", "gy", None),
            P("shot", None, "gx", "gy", None),
        ),
        check_vma=False,
    )
```

```python
import functools

import jax
import jax.numpy as jnp
from jax import lax
from jax.experimental import pallas as pl
from jax.experimental.pallas import tpu as pltpu
from jax.sharding import PartitionSpec as P

REC_Z = 8
STEPS = 4
LAPLACE_TAPS = (-205.0 / 72.0, 8.0 / 5.0, -1.0 / 5.0, 8.0 / 315.0, -1.0 / 560.0)
SLOPE_TAPS = (4.0 / 5.0, -1.0 / 5.0, 4.0 / 105.0, -1.0 / 280.0)


def y_plus(centre, halo, row, k):
    return pltpu.roll(jnp.where(row < k, halo, centre), 8 - k, 1)


def y_minus(centre, halo, row, k):
    return pltpu.roll(jnp.where(row >= 8 - k, halo, centre), k, 1)


def z_plus(lower, upper, lane, k):
    low, up = pltpu.roll(lower, 128 - k, 2), pltpu.roll(upper, 128 - k, 2)
    return jnp.where(lane < 128 - k, low, up), up


def z_minus(lower, upper, lane, k):
    low, up = pltpu.roll(lower, k, 2), pltpu.roll(upper, k, 2)
    return low, jnp.where(lane >= k, up, low)


def y_plus_outer(centre, above, below, row, k):
    return pltpu.roll(jnp.where(row < k, centre, jnp.where(row < k + 4, above, below)), 8 - k, 1)


def y_minus_outer(centre, above, below, row, k):
    return pltpu.roll(
        jnp.where(row >= 8 - k, centre, jnp.where(row < 4 - k, above, below)), k, 1
    )


def kernel(
    n_x,
    n_y,
    velocity,
    density,
    stored,
    holders,
    adjoint,
    traces,
    aperture,
    image_out,
    forward_out,
    adjoint_out,
    ahead,
    ahead_y,
    wide,
    below,
    above,
    corner,
    ring,
    mid,
    mid_y,
    old,
    back,
    back_y,
    back_old,
    last,
    part,
    coef,
    coef_y,
    dens,
    dens_ring,
    dens_far,
    speed,
    speed_y,
    pieces,
    holders_v,
    traces_v,
    aperture_v,
    inject,
    share,
    partner_share,
    small_sem,
    local_sem,
    own_sem,
    piece_sem,
    piece_send,
    model_send,
    model_recv,
    outer_send,
    outer_recv,
    hand_send,
    hand_recv,
    deep_send,
    deep_recv,
    ahead_send,
    ahead_recv,
    back_send,
    back_recv,
    image_sem,
    out_sem,
):
    s, b, j = lax.axis_index("shot"), lax.axis_index("gx"), lax.axis_index("gy")
    other = 1 - s
    f32 = jnp.float32

    smalls = [
        pltpu.make_async_copy(holders, holders_v, small_sem.at[0]),
        pltpu.make_async_copy(traces.at[0], traces_v, small_sem.at[1]),
        pltpu.make_async_copy(aperture, aperture_v, small_sem.at[2]),
    ]
    owns = [
        pltpu.make_async_copy(adjoint.at[0, 0], back.at[0, pl.ds(4, 8)], own_sem.at[0]),
        pltpu.make_async_copy(adjoint.at[0, 1], back_old, own_sem.at[1]),
    ]
    own_model = [
        pltpu.make_async_copy(density, dens.at[s, pl.ds(8, 8)], local_sem.at[0]),
        pltpu.make_async_copy(velocity, speed.at[s, pl.ds(4, 8)], local_sem.at[1]),
        pltpu.make_async_copy(stored.at[b], pieces.at[b], local_sem.at[2]),
    ]

    barrier = pltpu.get_barrier_semaphore()

    def greet(step, carry):
        pl.semaphore_signal(barrier, inc=1, device_id={"gx": lax.rem(b + step, n_x)})
        return carry

    lax.fori_loop(1, n_x, greet, 0)

    def toward(dx, dy, shot=None):
        target = {} if shot is None else {"shot": shot}
        if dx:
            target["gx"] = lax.rem(b + n_x + dx, n_x)
        if dy:
            target["gy"] = lax.rem(j + n_y + dy, n_y)
        return target

    sides = ((1, 0), (-1, 0), (0, 1), (0, -1))
    diagonals = ((1, 1), (1, -1), (-1, 1), (-1, -1))
    near = [{"shot": other}]
    near += [toward(0, dy) for dy in (1, -1)]
    near += [toward(dx, dy) for dx, dy in diagonals]
    near += [toward(dx, dy, other) for dx, dy in sides]
    for target in near:
        pl.semaphore_signal(barrier, inc=1, device_id=target)

    for copy in own_model + owns + smalls:
        copy.start()

    def fill(refs, value):
        for ref in refs:
            ref[...] = jnp.full(ref.shape, value, f32)

    low4, high4 = pl.ds(0, 4), pl.ds(4, 4)

    @pl.when(b == 0)
    def _():
        fill((wide.at[:8], corner.at[:4], ahead.at[:, :4], back.at[:, :4], speed.at[s, low4]), 0.0)
        fill((dens.at[:, 4:8],), 1.0)
        fill((dens.at[s, low4], dens_ring.at[s, low4]), 1.0)

    @pl.when(b == n_x - 1)
    def _():
        fill((wide.at[16:], corner.at[4:], ahead.at[:, 12:], back.at[:, 12:]), 0.0)
        fill((speed.at[s, pl.ds(12, 4)],), 0.0)
        fill((dens.at[:, 16:20],), 1.0)
        fill((dens.at[s, pl.ds(20, 4)], dens_ring.at[s, pl.ds(12, 4)]), 1.0)

    @pl.when(j == 0)
    def _():
        fill((below, corner.at[:, 4:], ahead_y.at[:, :, 4:], back_y.at[:, :, 4:]), 0.0)
        fill((speed_y.at[s, :, high4],), 0.0)
        fill((dens_ring.at[:, 4:12, 4:],), 1.0)
        fill((dens_far.at[s, :, low4], dens_ring.at[s, :, high4]), 1.0)

    @pl.when(j == n_y - 1)
    def _():
        fill((above, corner.at[:, :4], ahead_y.at[:, :, :4], back_y.at[:, :, :4]), 0.0)
        fill((speed_y.at[s, :, low4],), 0.0)
        fill((dens_ring.at[:, 4:12, :4],), 1.0)
        fill((dens_far.at[s, :, high4], dens_ring.at[s, :, low4]), 1.0)

    pl.semaphore_wait(barrier, n_x - 1 + len(near))

    def send_piece(step, carry):
        target = lax.rem(b + step, n_x)
        pltpu.make_async_remote_copy(
            stored.at[target], pieces.at[b], piece_send, piece_sem, device_id={"gx": target}
        ).start()
        return carry

    lax.fori_loop(1, n_x, send_piece, 0)

    def exists(dx, dy):
        there = b >= 0
        if dx:
            there &= (b < n_x - 1) if dx > 0 else (b > 0)
        if dy:
            there &= (j < n_y - 1) if dy > 0 else (j > 0)
        return there

    class Group:
        def __init__(self, entries, send_sem, recv_sem):
            self.items = []
            for at, (dx, dy, shot, src, dst) in enumerate(entries):
                copy = pltpu.make_async_remote_copy(
                    src, dst, send_sem.at[at], recv_sem.at[at], device_id=toward(dx, dy, shot)
                )
                self.items.append((copy, dx, dy))
            for copy, dx, dy in self.items:
                self.guard(dx, dy, copy.start)

        def guard(self, dx, dy, action):
            if dx or dy:
                pl.when(exists(dx, dy))(action)
            else:
                action()

        def received(self):
            for copy, dx, dy in self.items:
                self.guard(-dx, -dy, copy.wait_recv)

        def sent(self):
            for copy, dx, dy in self.items:
                self.guard(dx, dy, copy.wait_send)

    first, final = pl.ds(0, 4), pl.ds(4, 4)

    def shallow(src, base, planes, rows, shot=None):
        return [
            (1, 0, shot, src.at[pl.ds(base + 4, 4)], planes.at[pl.ds(0, 4)]),
            (-1, 0, shot, src.at[pl.ds(base, 4)], planes.at[pl.ds(12, 4)]),
            (0, 1, shot, src.at[pl.ds(base, 8), final], rows.at[:, final]),
            (0, -1, shot, src.at[pl.ds(base, 8), first], rows.at[:, first]),
        ]

    def deep(src, base, planes, lower, upper, corners, shot=None):
        whole = src.at[pl.ds(base, 8)]
        entries = [
            (1, 0, shot, whole, planes.at[pl.ds(0, 8)]),
            (-1, 0, shot, whole, planes.at[pl.ds(16, 8)]),
        ]
        for dx, dy in diagonals:
            rows = final if dy > 0 else first
            here = pl.ds(base + 4, 4) if dx > 0 else pl.ds(base, 4)
            there = first if dx > 0 else final
            entries.append((dx, dy, shot, src.at[here, rows], corners.at[there, rows]))
        entries.append((0, 1, shot, whole, lower))
        entries.append((0, -1, shot, whole, upper))
        return entries

    ring_s = dens_ring.at[s]
    model = [
        (0, 0, other, density, dens.at[s, pl.ds(8, 8)]),
        (0, 0, other, velocity, speed.at[s, pl.ds(4, 8)]),
    ]
    for shot in (None, other):
        model += shallow(density, 0, dens.at[s, pl.ds(4, 16)], ring_s.at[pl.ds(4, 8)], shot)
    model = Group(model, model_send, model_recv)
    backs = [
        Group(
            shallow(adjoint.at[0, 0], 0, back.at[0], back_y.at[0]), back_send.at[0], back_recv.at[0]
        )
    ]

    outer_model = shallow(velocity, 0, speed.at[s], speed_y.at[s])
    outer_model += [
        (1, 0, None, density.at[first], dens.at[s, pl.ds(0, 4)]),
        (-1, 0, None, density.at[final], dens.at[s, pl.ds(20, 4)]),
        (0, 1, None, density.at[:, first], dens_far.at[s, :, first]),
        (0, -1, None, density.at[:, final], dens_far.at[s, :, final]),
    ]
    for dx, dy in diagonals:
        rows = final if dy > 0 else first
        here, there = (final, first) if dx > 0 else (first, pl.ds(12, 4))
        outer_model.append((dx, dy, None, density.at[here, rows], ring_s.at[there, rows]))
    groups = [model]

    row = lax.broadcasted_iota(jnp.int32, (1, 8, 128), 1)
    lane = lax.broadcasted_iota(jnp.int32, (1, 8, 128), 2)
    halves = (pl.ds(0, 128), pl.ds(128, 128))

    for copy in smalls:
        copy.wait()
    column = lax.broadcasted_iota(jnp.int32, (64, n_x), 0)
    place = column // 2
    parity = column - 2 * place
    hit = holders_v[...] == place
    picks = [jnp.where(hit & (parity == r), 1.0, 0.0).astype(f32) for r in range(2)]

    bounds = aperture_v[...]
    bounds = jnp.where(s == 0, bounds[0:1], bounds[1:2])
    active = jnp.where((b >= bounds[:, 0:1]) & (b < bounds[:, 1:2]), 1.0, 0.0).astype(f32)
    active = active.reshape(1, 1, 1)

    def coefficients(out, parts, speeds, logs, x_of, plus_of, minus_of):
        def put(at, lanes, value):
            start = 0
            for low, count in parts:
                out[at, low : low + count, :, lanes] = value[start : start + count]
                start += count

        grads = [[0.0, 0.0, 0.0] for half in range(2)]
        for k in range(1, 5):
            tap = SLOPE_TAPS[k - 1]
            ahead = z_plus(logs[0], logs[1], lane, k)
            behind = z_minus(logs[0], logs[1], lane, k)
            ahead = (ahead[0], jnp.where(lane < 128 - k, ahead[1], 0.0))
            behind = (jnp.where(lane >= k, behind[0], 0.0), behind[1])
            for half in range(2):
                grads[half][0] += tap * (x_of(half, k) - x_of(half, -k))
                grads[half][1] += tap * (plus_of(half, k) - minus_of(half, k))
                grads[half][2] += tap * (ahead[half] - behind[half])
        for half, lanes in enumerate(halves):
            sq = speeds(half)
            sq = sq * sq
            put(0, lanes, 2.0 + (3.0 * LAPLACE_TAPS[0]) * sq)
            slopes = [sq * grad for grad in grads[half]]
            for k in range(1, 5):
                even = LAPLACE_TAPS[k] * sq
                for axis in range(3):
                    odd = SLOPE_TAPS[k - 1] * slopes[axis]
                    plus, minus = even - odd, even + odd
                    if axis == 2 and half == 0:
                        minus = jnp.where(lane >= k, minus, 0.0)
                    elif axis == 2:
                        plus = jnp.where(lane < 128 - k, plus, 0.0)
                    at = 1 + 6 * (k - 1) + 2 * axis
                    put(at, lanes, plus)
                    put(at + 1, lanes, minus)

    def steps(count, table, base, centre_of, x_of, plus_of, minus_of, before_of, put):
        def one(p, carry):
            centre = [centre_of(p, lanes) for lanes in halves]
            place = pl.ds(base + p, 1)
            total = [
                table[0, place, :, lanes] * centre[half] - before_of(p, lanes)
                for half, lanes in enumerate(halves)
            ]
            for k in range(1, 5):
                at = 1 + 6 * (k - 1)
                up = z_plus(centre[0], centre[1], lane, k)
                down = z_minus(centre[0], centre[1], lane, k)
                for half, lanes in enumerate(halves):
                    total[half] = (
                        total[half]
                        + table[at, place, :, lanes] * x_of(p, lanes, k)
                        + table[at + 1, place, :, lanes] * x_of(p, lanes, -k)
                        + table[at + 2, place, :, lanes] * plus_of(p, lanes, centre[half], k)
                        + table[at + 3, place, :, lanes] * minus_of(p, lanes, centre[half], k)
                        + table[at + 4, place, :, lanes] * up[half]
                        + table[at + 5, place, :, lanes] * down[half]
                    )
            for half, lanes in enumerate(halves):
                put(p, lanes, total[half], half)
            return carry

        lax.fori_loop(0, count, one, 0, unroll=True)

    def into(ref, base):
        def put(p, lanes, value, half):
            ref[pl.ds(base + p, 1), :, lanes] = value

        return put

    def plane_of(ref, base):
        return lambda p, lanes, k=0: ref[pl.ds(base + p + k, 1), :, lanes]

    def inner_step(planes, rows, before, put, base=4, first_row=0):
        edge = plane_of(rows, first_row)
        steps(
            8,
            coef,
            base,
            plane_of(planes, base),
            plane_of(planes, base),
            lambda p, lanes, centre, k: y_plus(centre, edge(p, lanes), row, k),
            lambda p, lanes, centre, k: y_minus(centre, edge(p, lanes), row, k),
            before,
            put,
        )

    def begin_step(planes, base, before):
        own = plane_of(planes, base)

        def one(p, carry):
            centre = [own(p, lanes) for lanes in halves]
            place = pl.ds(4 + p, 1)
            total = [
                coef[0, place, :, lanes] * centre[half] - before(p, lanes)
                for half, lanes in enumerate(halves)
            ]
            for k in range(1, 5):
                at = 1 + 6 * (k - 1)
                up = z_plus(centre[0], centre[1], lane, k)
                down = z_minus(centre[0], centre[1], lane, k)
                for half, lanes in enumerate(halves):
                    plus = jnp.where(row < 8 - k, pltpu.roll(centre[half], 8 - k, 1), 0.0)
                    minus = jnp.where(row >= k, pltpu.roll(centre[half], k, 1), 0.0)
                    total[half] = (
                        total[half]
                        + coef[at + 2, place, :, lanes] * plus
                        + coef[at + 3, place, :, lanes] * minus
                        + coef[at + 4, place, :, lanes] * up[half]
                        + coef[at + 5, place, :, lanes] * down[half]
                    )
            for half, lanes in enumerate(halves):
                part[pl.ds(p, 1), :, lanes] = total[half]
            return carry

        lax.fori_loop(0, 8, one, 0, unroll=True)

    def end_step(planes, base, edge, put):
        own = plane_of(planes, base)

        def one(p, carry):
            place = pl.ds(4 + p, 1)
            for half, lanes in enumerate(halves):
                total = part[pl.ds(p, 1), :, lanes]
                around = edge(p, lanes)
                for k in range(1, 5):
                    at = 1 + 6 * (k - 1)
                    plus = jnp.where(row >= 8 - k, pltpu.roll(around, 8 - k, 1), 0.0)
                    minus = jnp.where(row < k, pltpu.roll(around, k, 1), 0.0)
                    total = (
                        total
                        + coef[at, place, :, lanes] * own(p, lanes, k)
                        + coef[at + 1, place, :, lanes] * own(p, lanes, -k)
                        + coef[at + 2, place, :, lanes] * plus
                        + coef[at + 3, place, :, lanes] * minus
                    )
                put(p, lanes, total, half)
            return carry

        lax.fori_loop(0, 8, one, 0, unroll=True)

    def back_step(level):
        backs[level].received()
        before = plane_of(back_old, 0) if level == 0 else plane_of(back.at[level - 1], 4)
        target = last.at[1] if level == STEPS - 1 else back.at[level + 1]
        start = 0 if level == STEPS - 1 else 4

        def put(p, lanes, value, half):
            if half == 0:
                value = value + inject[STEPS - 1 - level, pl.ds(p, 1)]
            target[pl.ds(start + p, 1), :, lanes] = value

        inner_step(back.at[level], back_y.at[level], before, put)
        if level < STEPS - 1:
            backs.append(
                Group(
                    shallow(back.at[level + 1], 4, back.at[level + 1], back_y.at[level + 1]),
                    back_send.at[level + 1],
                    back_recv.at[level + 1],
                )
            )

    def send_ahead(level):
        group = Group(
            shallow(ahead.at[level], 4, ahead.at[level], ahead_y.at[level]),
            ahead_send.at[level],
            ahead_recv.at[level],
        )
        groups.append(group)
        return group

    outer_model = Group(outer_model, outer_send, outer_recv)
    groups.append(outer_model)

    own_model[2].wait()
    arrived = pieces.at[pl.ds(0, n_x - 1)]
    pltpu.make_async_copy(arrived, arrived, piece_sem).wait()
    for level in (0, 1):
        found = 0.0
        for r in range(2):
            found += jnp.dot(
                picks[r],
                pieces[:, level, r, :],
                precision=lax.Precision.HIGHEST,
                preferred_element_type=f32,
            )
        found = found.reshape(8, 8, 256)
        if level == 0:
            ahead[0, 4:12] = found
            exchange = send_ahead(0)
        else:
            old[...] = found

    for copy in own_model[:2]:
        copy.wait()
    model.received()
    for half in range(2):
        dens[half, 4:20] = jnp.log(dens[half, 4:20])
        dens_ring[half, 4:12] = jnp.log(dens_ring[half, 4:12])
    coefficients(
        coef,
        ((4, 8),),
        lambda half: speed[half, 4:12],
        [dens[half, 8:16] for half in range(2)],
        lambda half, k: dens[half, 8 + k : 16 + k],
        lambda half, k: y_plus(dens[half, 8:16], dens_ring[half, 4:12], row, k),
        lambda half, k: y_minus(dens[half, 8:16], dens_ring[half, 4:12], row, k),
    )
    eye = lax.broadcasted_iota(jnp.int32, (8, 8), 0) == lax.broadcasted_iota(jnp.int32, (8, 8), 1)
    at_receiver = lax.broadcasted_iota(jnp.int32, (8, 128), 1) == REC_Z
    for x in range(8):
        sq = speed[0, 4 + x] * speed[0, 4 + x]
        for number in range(STEPS):
            line = jnp.where(eye, traces_v[number, pl.ds(x, 1), :], 0.0)
            line = jnp.sum(line, axis=1, keepdims=True)
            inject[number, x] = jnp.where(at_receiver, line, 0.0) * sq

    for copy in owns:
        copy.wait()
    back_step(0)

    begin_step(ahead.at[0], 4, plane_of(old, 0))
    exchange.received()
    end_step(ahead.at[0], 4, plane_of(ahead_y.at[0], 0), into(ahead.at[1], 4))
    exchange = send_ahead(1)
    outer_model.received()
    for planes in (pl.ds(0, 4), pl.ds(20, 4)):
        dens[s, planes] = jnp.log(dens[s, planes])
    for planes in (pl.ds(0, 4), pl.ds(12, 4)):
        dens_ring[s, planes] = jnp.log(dens_ring[s, planes])
    dens_far[s] = jnp.log(dens_far[s])
    handed = [
        ref.at[s, pl.ds(start, count)]
        for ref, start, count in (
            (speed, 0, 4),
            (speed, 12, 4),
            (speed_y, 0, 8),
            (dens, 0, 4),
            (dens, 20, 4),
            (dens_ring, 0, 4),
            (dens_ring, 12, 4),
            (dens_far, 0, 8),
        )
    ]
    handed = Group([(0, 0, other, ref, ref) for ref in handed], hand_send, hand_recv)
    groups.append(handed)
    back_step(1)
    begin_step(ahead.at[1], 4, plane_of(ahead.at[0], 4))
    exchange.received()
    end_step(ahead.at[1], 4, plane_of(ahead_y.at[1], 0), into(wide, 8))
    exchange = Group(deep(wide, 8, wide, below, above, corner), deep_send, deep_recv)
    groups.append(exchange)

    back_step(2)
    handed.received()

    def both(ref, half, low, high):
        return jnp.concatenate([ref[half, low : low + 4], ref[half, high : high + 4]], axis=0)

    coefficients(
        coef,
        ((0, 4), (12, 4)),
        lambda half: both(speed, half, 0, 12),
        [both(dens, half, 4, 16) for half in range(2)],
        lambda half, k: both(dens, half, 4 + k, 16 + k),
        lambda half, k: y_plus(both(dens, half, 4, 16), both(dens_ring, half, 0, 12), row, k),
        lambda half, k: y_minus(both(dens, half, 4, 16), both(dens_ring, half, 0, 12), row, k),
    )
    dens_above = [
        jnp.where(row < 4, dens_ring[half, 4:12], dens_far[half]) for half in range(2)
    ]
    dens_below = [
        jnp.where(row < 4, dens_far[half], dens_ring[half, 4:12]) for half in range(2)
    ]
    coefficients(
        coef_y,
        ((0, 8),),
        lambda half: speed_y[half],
        [dens_ring[half, 4:12] for half in range(2)],
        lambda half, k: dens_ring[half, 4 + k : 12 + k],
        lambda half, k: y_plus_outer(dens[half, 8:16], dens_above[half], dens_below[half], row, k),
        lambda half, k: y_minus_outer(dens[half, 8:16], dens_above[half], dens_below[half], row, k),
    )

    outs = [pltpu.make_async_copy(back.at[3, pl.ds(4, 8)], adjoint_out.at[0, 1], out_sem.at[0])]
    outs[0].start()
    early = [
        ahead[1, 4:12, :, lanes] * back[3, 4:12, :, lanes]
        + wide[8:16, :, lanes] * back[2, 4:12, :, lanes]
        for lanes in halves
    ]

    begin_step(wide, 8, plane_of(ahead.at[1], 4))
    exchange.received()
    for lanes in halves:
        ring[0:4, :, lanes] = corner[0:4, :, lanes]
        ring[4:12, :, lanes] = jnp.where(row < 4, above[:, :, lanes], below[:, :, lanes])
        ring[12:16, :, lanes] = corner[4:8, :, lanes]
    low, mine, up = plane_of(below, 0), plane_of(wide, 8), plane_of(above, 0)
    steps(
        8,
        coef_y,
        0,
        plane_of(ring, 4),
        plane_of(ring, 4),
        lambda p, lanes, centre, k: y_plus_outer(
            mine(p, lanes), up(p, lanes), low(p, lanes), row, k
        ),
        lambda p, lanes, centre, k: y_minus_outer(
            mine(p, lanes), up(p, lanes), low(p, lanes), row, k
        ),
        plane_of(ahead_y.at[1], 0),
        into(mid_y, 0),
    )
    for start in (0, 12):
        around = plane_of(ring, start)
        steps(
            4,
            coef,
            start,
            plane_of(wide, 4 + start),
            plane_of(wide, 4 + start),
            lambda p, lanes, centre, k: y_plus(centre, around(p, lanes), row, k),
            lambda p, lanes, centre, k: y_minus(centre, around(p, lanes), row, k),
            plane_of(ahead.at[1], start),
            into(mid, start),
        )
    end_step(wide, 8, plane_of(ring, 4), into(mid, 4))
    outs.append(pltpu.make_async_copy(mid.at[pl.ds(4, 8)], forward_out.at[0, 1], out_sem.at[1]))
    outs[1].start()
    inner_step(mid, mid_y, plane_of(wide, 8), into(last.at[0], 0))
    whole = [
        active
        * (
            early[half]
            + mid[4:12, :, lanes] * back[1, 4:12, :, lanes]
            + last[0, :, :, lanes] * back[0, 4:12, :, lanes]
        )
        for half, lanes in enumerate(halves)
    ]
    share[...] = jnp.where(s == 0, whole[1], whole[0])
    to_partner = pltpu.make_async_remote_copy(
        share, partner_share, image_sem.at[0], image_sem.at[1], device_id={"shot": other}
    )
    to_partner.start()
    outs.append(pltpu.make_async_copy(last.at[0], forward_out.at[0, 0], out_sem.at[2]))
    outs[2].start()
    image_out[...] = jnp.where(s == 0, whole[0], whole[1])

    back_step(3)
    outs.append(pltpu.make_async_copy(last.at[1], adjoint_out.at[0, 0], out_sem.at[3]))
    outs[3].start()

    gone = stored.at[pl.ds(0, n_x - 1)]
    pltpu.make_async_copy(gone, gone, piece_send).wait()
    for group in groups + backs:
        group.sent()

    to_partner.wait()
    image_out[...] += partner_share[...]
    for copy in outs:
        copy.wait()


def finish(image, forward, adjoint, image_out, forward_out, adjoint_out, sem):
    copies = [
        pltpu.make_async_copy(src, dst, sem.at[at])
        for at, (src, dst) in enumerate(
            ((image, image_out), (forward, forward_out), (adjoint, adjoint_out))
        )
    ]
    for copy in copies:
        copy.start()
    for copy in copies:
        copy.wait()


def shards(n_x, n_y, velocity, density, stored, holders, adjoint, traces, aperture):
    f32 = jnp.float32
    anywhere = pl.BlockSpec(memory_space=pl.ANY)
    inside = pl.BlockSpec(memory_space=pltpu.VMEM)
    results = pl.pallas_call(
        functools.partial(kernel, n_x, n_y),
        out_shape=(
            pltpu.VMEM((8, 8, 128), f32),
            pltpu.VMEM((1, 2, 8, 8, 256), f32),
            pltpu.VMEM((1, 2, 8, 8, 256), f32),
        ),
        in_specs=[anywhere] * 7,
        out_specs=(inside,) * 3,
        scratch_shapes=[
            pltpu.VMEM((2, 16, 8, 256), f32),
            pltpu.VMEM((2, 8, 8, 256), f32),
            pltpu.VMEM((24, 8, 256), f32),
            pltpu.VMEM((8, 8, 256), f32),
            pltpu.VMEM((8, 8, 256), f32),
            pltpu.VMEM((8, 8, 256), f32),
            pltpu.VMEM((16, 8, 256), f32),
            pltpu.VMEM((16, 8, 256), f32),
            pltpu.VMEM((8, 8, 256), f32),
            pltpu.VMEM((8, 8, 256), f32),
            pltpu.VMEM((STEPS, 16, 8, 256), f32),
            pltpu.VMEM((STEPS, 8, 8, 256), f32),
            pltpu.VMEM((8, 8, 256), f32),
            pltpu.VMEM((2, 8, 8, 256), f32),
            pltpu.VMEM((8, 8, 256), f32),
            pltpu.VMEM((25, 16, 8, 256), f32),
            pltpu.VMEM((25, 8, 8, 256), f32),
            pltpu.VMEM((2, 24, 8, 128), f32),
            pltpu.VMEM((2, 16, 8, 128), f32),
            pltpu.VMEM((2, 8, 8, 128), f32),
            pltpu.VMEM((2, 16, 8, 128), f32),
            pltpu.VMEM((2, 8, 8, 128), f32),
            pltpu.VMEM((n_x, 2, 2, 256), f32),
            pltpu.VMEM((1, n_x), jnp.int32),
            pltpu.VMEM((STEPS, 8, 8), f32),
            pltpu.VMEM((2, 2), jnp.int32),
            pltpu.VMEM((STEPS, 8, 8, 128), f32),
            pltpu.VMEM((8, 8, 128), f32),
            pltpu.VMEM((8, 8, 128), f32),
            pltpu.SemaphoreType.DMA((3,)),
            pltpu.SemaphoreType.DMA((3,)),
            pltpu.SemaphoreType.DMA((2,)),
            pltpu.SemaphoreType.DMA,
            pltpu.SemaphoreType.DMA,
            pltpu.SemaphoreType.DMA((10,)),
            pltpu.SemaphoreType.DMA((10,)),
            pltpu.SemaphoreType.DMA((12,)),
            pltpu.SemaphoreType.DMA((12,)),
            pltpu.SemaphoreType.DMA((8,)),
            pltpu.SemaphoreType.DMA((8,)),
            pltpu.SemaphoreType.DMA((8,)),
            pltpu.SemaphoreType.DMA((8,)),
            pltpu.SemaphoreType.DMA((2, 4)),
            pltpu.SemaphoreType.DMA((2, 4)),
            pltpu.SemaphoreType.DMA((STEPS, 4)),
            pltpu.SemaphoreType.DMA((STEPS, 4)),
            pltpu.SemaphoreType.DMA((2,)),
            pltpu.SemaphoreType.DMA((4,)),
        ],
        compiler_params=pltpu.CompilerParams(
            collective_id=0, has_side_effects=True, vmem_limit_bytes=48 * 1024 * 1024
        ),
        cost_estimate=pl.CostEstimate(flops=8_000_000, bytes_accessed=800_000, transcendentals=0),
    )(*(
        pltpu.with_memory_space_constraint(given, pltpu.HBM)
        for given in (velocity, density, stored, holders, adjoint, traces, aperture)
    ))
    return pl.pallas_call(
        finish,
        out_shape=tuple(jax.ShapeDtypeStruct(one.shape, f32) for one in results),
        in_specs=[inside] * 3,
        out_specs=(anywhere,) * 3,
        scratch_shapes=[pltpu.SemaphoreType.DMA((3,))],
    )(*(pltpu.with_memory_space_constraint(one, pltpu.VMEM) for one in results))


def solution(mesh):
    return jax.shard_map(
        functools.partial(shards, mesh.shape["gx"], mesh.shape["gy"]),
        mesh=mesh,
        in_specs=(
            P("gx", "gy", "shot"),
            P("gx", "gy", "shot"),
            P("gx", None, ("shot", "gy"), None),
            P("gx", None),
            P("shot", None, "gx", "gy", None),
            P("shot", None, "gx", "gy"),
            P(),
        ),
        out_specs=(
            P("gx", "gy", "shot"),
            P("shot", None, "gx", "gy", None),
            P("shot", None, "gx", "gy", None),
        ),
        check_vma=False,
    )
```

```python
import functools

import jax
import jax.numpy as jnp
from jax import lax
from jax.experimental import pallas as pl
from jax.experimental.pallas import tpu as pltpu
from jax.sharding import PartitionSpec as P

REC_Z = 8
STEPS = 4
LAPLACE_TAPS = (-205.0 / 72.0, 8.0 / 5.0, -1.0 / 5.0, 8.0 / 315.0, -1.0 / 560.0)
SLOPE_TAPS = (4.0 / 5.0, -1.0 / 5.0, 4.0 / 105.0, -1.0 / 280.0)


def y_plus(centre, halo, row, k):
    return pltpu.roll(jnp.where(row < k, halo, centre), 8 - k, 1)


def y_minus(centre, halo, row, k):
    return pltpu.roll(jnp.where(row >= 8 - k, halo, centre), k, 1)


def z_plus(lower, upper, lane, k):
    low, up = pltpu.roll(lower, 128 - k, 2), pltpu.roll(upper, 128 - k, 2)
    return jnp.where(lane < 128 - k, low, up), up


def z_minus(lower, upper, lane, k):
    low, up = pltpu.roll(lower, k, 2), pltpu.roll(upper, k, 2)
    return low, jnp.where(lane >= k, up, low)


def y_plus_outer(centre, above, below, row, k):
    return pltpu.roll(jnp.where(row < k, centre, jnp.where(row < k + 4, above, below)), 8 - k, 1)


def y_minus_outer(centre, above, below, row, k):
    return pltpu.roll(
        jnp.where(row >= 8 - k, centre, jnp.where(row < 4 - k, above, below)), k, 1
    )


def kernel(
    n_x,
    n_y,
    velocity,
    density,
    stored,
    holders,
    adjoint,
    traces,
    aperture,
    image_out,
    forward_out,
    adjoint_out,
    ahead,
    ahead_y,
    wide,
    below,
    above,
    corner,
    ring,
    mid,
    mid_y,
    old,
    back,
    back_y,
    back_old,
    last,
    part,
    coef,
    coef_y,
    dens,
    dens_ring,
    dens_far,
    speed,
    speed_y,
    pieces,
    holders_v,
    traces_v,
    aperture_v,
    inject,
    share,
    partner_share,
    small_sem,
    local_sem,
    own_sem,
    piece_sem,
    piece_send,
    model_send,
    model_recv,
    outer_send,
    outer_recv,
    hand_send,
    hand_recv,
    deep_send,
    deep_recv,
    ahead_send,
    ahead_recv,
    back_send,
    back_recv,
    image_sem,
    out_sem,
):
    s, b, j = lax.axis_index("shot"), lax.axis_index("gx"), lax.axis_index("gy")
    other = 1 - s
    f32 = jnp.float32

    smalls = [
        pltpu.make_async_copy(holders, holders_v, small_sem.at[0]),
        pltpu.make_async_copy(traces.at[0], traces_v, small_sem.at[1]),
        pltpu.make_async_copy(aperture, aperture_v, small_sem.at[2]),
    ]
    owns = [
        pltpu.make_async_copy(adjoint.at[0, 0], back.at[0, pl.ds(4, 8)], own_sem.at[0]),
        pltpu.make_async_copy(adjoint.at[0, 1], back_old, own_sem.at[1]),
    ]
    own_model = [
        pltpu.make_async_copy(density, dens.at[s, pl.ds(8, 8)], local_sem.at[0]),
        pltpu.make_async_copy(velocity, speed.at[s, pl.ds(4, 8)], local_sem.at[1]),
        pltpu.make_async_copy(stored.at[b], pieces.at[b], local_sem.at[2]),
    ]

    barrier = pltpu.get_barrier_semaphore()

    def greet(step, carry):
        pl.semaphore_signal(barrier, inc=1, device_id={"gx": lax.rem(b + step, n_x)})
        return carry

    lax.fori_loop(1, n_x, greet, 0)

    def toward(dx, dy, shot=None):
        target = {} if shot is None else {"shot": shot}
        if dx:
            target["gx"] = lax.rem(b + n_x + dx, n_x)
        if dy:
            target["gy"] = lax.rem(j + n_y + dy, n_y)
        return target

    sides = ((1, 0), (-1, 0), (0, 1), (0, -1))
    diagonals = ((1, 1), (1, -1), (-1, 1), (-1, -1))
    near = [{"shot": other}]
    near += [toward(0, dy) for dy in (1, -1)]
    near += [toward(dx, dy) for dx, dy in diagonals]
    near += [toward(dx, dy, other) for dx, dy in sides]
    for target in near:
        pl.semaphore_signal(barrier, inc=1, device_id=target)

    for copy in own_model + owns + smalls:
        copy.start()

    def fill(refs, value):
        for ref in refs:
            ref[...] = jnp.full(ref.shape, value, f32)

    low4, high4 = pl.ds(0, 4), pl.ds(4, 4)

    @pl.when(b == 0)
    def _():
        fill((wide.at[:8], corner.at[:4], ahead.at[:, :4], back.at[:, :4], speed.at[s, low4]), 0.0)
        fill((dens.at[:, 4:8],), 1.0)
        fill((dens.at[s, low4], dens_ring.at[s, low4]), 1.0)

    @pl.when(b == n_x - 1)
    def _():
        fill((wide.at[16:], corner.at[4:], ahead.at[:, 12:], back.at[:, 12:]), 0.0)
        fill((speed.at[s, pl.ds(12, 4)],), 0.0)
        fill((dens.at[:, 16:20],), 1.0)
        fill((dens.at[s, pl.ds(20, 4)], dens_ring.at[s, pl.ds(12, 4)]), 1.0)

    @pl.when(j == 0)
    def _():
        fill((below, corner.at[:, 4:], ahead_y.at[:, :, 4:], back_y.at[:, :, 4:]), 0.0)
        fill((speed_y.at[s, :, high4],), 0.0)
        fill((dens_ring.at[:, 4:12, 4:],), 1.0)
        fill((dens_far.at[s, :, low4], dens_ring.at[s, :, high4]), 1.0)

    @pl.when(j == n_y - 1)
    def _():
        fill((above, corner.at[:, :4], ahead_y.at[:, :, :4], back_y.at[:, :, :4]), 0.0)
        fill((speed_y.at[s, :, low4],), 0.0)
        fill((dens_ring.at[:, 4:12, :4],), 1.0)
        fill((dens_far.at[s, :, high4], dens_ring.at[s, :, low4]), 1.0)

    pl.semaphore_wait(barrier, n_x - 1 + len(near))

    def send_piece(step, carry):
        target = lax.rem(b + step, n_x)
        pltpu.make_async_remote_copy(
            stored.at[target], pieces.at[b], piece_send, piece_sem, device_id={"gx": target}
        ).start()
        return carry

    lax.fori_loop(1, n_x, send_piece, 0)

    def exists(dx, dy):
        there = b >= 0
        if dx:
            there &= (b < n_x - 1) if dx > 0 else (b > 0)
        if dy:
            there &= (j < n_y - 1) if dy > 0 else (j > 0)
        return there

    class Group:
        def __init__(self, entries, send_sem, recv_sem):
            self.items = []
            for at, (dx, dy, shot, src, dst) in enumerate(entries):
                copy = pltpu.make_async_remote_copy(
                    src, dst, send_sem.at[at], recv_sem.at[at], device_id=toward(dx, dy, shot)
                )
                self.items.append((copy, dx, dy))
            for copy, dx, dy in self.items:
                self.guard(dx, dy, copy.start)

        def guard(self, dx, dy, action):
            if dx or dy:
                pl.when(exists(dx, dy))(action)
            else:
                action()

        def received(self):
            for copy, dx, dy in self.items:
                self.guard(-dx, -dy, copy.wait_recv)

        def sent(self):
            for copy, dx, dy in self.items:
                self.guard(dx, dy, copy.wait_send)

    first, final = pl.ds(0, 4), pl.ds(4, 4)

    def shallow(src, base, planes, rows, shot=None):
        return [
            (1, 0, shot, src.at[pl.ds(base + 4, 4)], planes.at[pl.ds(0, 4)]),
            (-1, 0, shot, src.at[pl.ds(base, 4)], planes.at[pl.ds(12, 4)]),
            (0, 1, shot, src.at[pl.ds(base, 8), final], rows.at[:, final]),
            (0, -1, shot, src.at[pl.ds(base, 8), first], rows.at[:, first]),
        ]

    def deep(src, base, planes, lower, upper, corners, shot=None):
        whole = src.at[pl.ds(base, 8)]
        entries = [
            (1, 0, shot, whole, planes.at[pl.ds(0, 8)]),
            (-1, 0, shot, whole, planes.at[pl.ds(16, 8)]),
        ]
        for dx, dy in diagonals:
            rows = final if dy > 0 else first
            here = pl.ds(base + 4, 4) if dx > 0 else pl.ds(base, 4)
            there = first if dx > 0 else final
            entries.append((dx, dy, shot, src.at[here, rows], corners.at[there, rows]))
        entries.append((0, 1, shot, whole, lower))
        entries.append((0, -1, shot, whole, upper))
        return entries

    ring_s = dens_ring.at[s]
    model = [
        (0, 0, other, density, dens.at[s, pl.ds(8, 8)]),
        (0, 0, other, velocity, speed.at[s, pl.ds(4, 8)]),
    ]
    for shot in (None, other):
        model += shallow(density, 0, dens.at[s, pl.ds(4, 16)], ring_s.at[pl.ds(4, 8)], shot)
    model = Group(model, model_send, model_recv)
    backs = [
        Group(
            shallow(adjoint.at[0, 0], 0, back.at[0], back_y.at[0]), back_send.at[0], back_recv.at[0]
        )
    ]

    outer_model = shallow(velocity, 0, speed.at[s], speed_y.at[s])
    outer_model += [
        (1, 0, None, density.at[first], dens.at[s, pl.ds(0, 4)]),
        (-1, 0, None, density.at[final], dens.at[s, pl.ds(20, 4)]),
        (0, 1, None, density.at[:, first], dens_far.at[s, :, first]),
        (0, -1, None, density.at[:, final], dens_far.at[s, :, final]),
    ]
    for dx, dy in diagonals:
        rows = final if dy > 0 else first
        here, there = (final, first) if dx > 0 else (first, pl.ds(12, 4))
        outer_model.append((dx, dy, None, density.at[here, rows], ring_s.at[there, rows]))
    groups = [model]

    row = lax.broadcasted_iota(jnp.int32, (1, 8, 128), 1)
    lane = lax.broadcasted_iota(jnp.int32, (1, 8, 128), 2)
    halves = (pl.ds(0, 128), pl.ds(128, 128))

    for copy in smalls:
        copy.wait()
    column = lax.broadcasted_iota(jnp.int32, (64, n_x), 0)
    place = column // 2
    parity = column - 2 * place
    hit = holders_v[...] == place
    picks = [jnp.where(hit & (parity == r), 1.0, 0.0).astype(f32) for r in range(2)]

    bounds = aperture_v[...]
    bounds = jnp.where(s == 0, bounds[0:1], bounds[1:2])
    active = jnp.where((b >= bounds[:, 0:1]) & (b < bounds[:, 1:2]), 1.0, 0.0).astype(f32)
    active = active.reshape(1, 1, 1)

    def coefficients(out, parts, speeds, logs, x_of, plus_of, minus_of):
        def put(at, lanes, value):
            start = 0
            for low, count in parts:
                out[at, low : low + count, :, lanes] = value[start : start + count]
                start += count

        grads = [[0.0, 0.0, 0.0] for half in range(2)]
        for k in range(1, 5):
            tap = SLOPE_TAPS[k - 1]
            ahead = z_plus(logs[0], logs[1], lane, k)
            behind = z_minus(logs[0], logs[1], lane, k)
            ahead = (ahead[0], jnp.where(lane < 128 - k, ahead[1], 0.0))
            behind = (jnp.where(lane >= k, behind[0], 0.0), behind[1])
            for half in range(2):
                grads[half][0] += tap * (x_of(half, k) - x_of(half, -k))
                grads[half][1] += tap * (plus_of(half, k) - minus_of(half, k))
                grads[half][2] += tap * (ahead[half] - behind[half])
        for half, lanes in enumerate(halves):
            sq = speeds(half)
            sq = sq * sq
            put(0, lanes, 2.0 + (3.0 * LAPLACE_TAPS[0]) * sq)
            slopes = [sq * grad for grad in grads[half]]
            for k in range(1, 5):
                even = LAPLACE_TAPS[k] * sq
                for axis in range(3):
                    odd = SLOPE_TAPS[k - 1] * slopes[axis]
                    plus, minus = even - odd, even + odd
                    if axis == 2 and half == 0:
                        minus = jnp.where(lane >= k, minus, 0.0)
                    elif axis == 2:
                        plus = jnp.where(lane < 128 - k, plus, 0.0)
                    at = 1 + 6 * (k - 1) + 2 * axis
                    put(at, lanes, plus)
                    put(at + 1, lanes, minus)

    def steps(count, table, base, centre_of, x_of, plus_of, minus_of, before_of, put):
        def one(p, carry):
            centre = [centre_of(p, lanes) for lanes in halves]
            place = pl.ds(base + p, 1)
            total = [
                table[0, place, :, lanes] * centre[half] - before_of(p, lanes)
                for half, lanes in enumerate(halves)
            ]
            for k in range(1, 5):
                at = 1 + 6 * (k - 1)
                up = z_plus(centre[0], centre[1], lane, k)
                down = z_minus(centre[0], centre[1], lane, k)
                for half, lanes in enumerate(halves):
                    total[half] = (
                        total[half]
                        + table[at, place, :, lanes] * x_of(p, lanes, k)
                        + table[at + 1, place, :, lanes] * x_of(p, lanes, -k)
                        + table[at + 2, place, :, lanes] * plus_of(p, lanes, centre[half], k)
                        + table[at + 3, place, :, lanes] * minus_of(p, lanes, centre[half], k)
                        + table[at + 4, place, :, lanes] * up[half]
                        + table[at + 5, place, :, lanes] * down[half]
                    )
            for half, lanes in enumerate(halves):
                put(p, lanes, total[half], half)
            return carry

        lax.fori_loop(0, count, one, 0, unroll=True)

    def into(ref, base):
        def put(p, lanes, value, half):
            ref[pl.ds(base + p, 1), :, lanes] = value

        return put

    def plane_of(ref, base):
        return lambda p, lanes, k=0: ref[pl.ds(base + p + k, 1), :, lanes]

    def inner_step(planes, rows, before, put, base=4, first_row=0):
        edge = plane_of(rows, first_row)
        steps(
            8,
            coef,
            base,
            plane_of(planes, base),
            plane_of(planes, base),
            lambda p, lanes, centre, k: y_plus(centre, edge(p, lanes), row, k),
            lambda p, lanes, centre, k: y_minus(centre, edge(p, lanes), row, k),
            before,
            put,
        )

    def begin_step(planes, base, before):
        own = plane_of(planes, base)

        def one(p, carry):
            centre = [own(p, lanes) for lanes in halves]
            place = pl.ds(4 + p, 1)
            total = [
                coef[0, place, :, lanes] * centre[half] - before(p, lanes)
                for half, lanes in enumerate(halves)
            ]
            for k in range(1, 5):
                at = 1 + 6 * (k - 1)
                up = z_plus(centre[0], centre[1], lane, k)
                down = z_minus(centre[0], centre[1], lane, k)
                for half, lanes in enumerate(halves):
                    plus = jnp.where(row < 8 - k, pltpu.roll(centre[half], 8 - k, 1), 0.0)
                    minus = jnp.where(row >= k, pltpu.roll(centre[half], k, 1), 0.0)
                    total[half] = (
                        total[half]
                        + coef[at + 2, place, :, lanes] * plus
                        + coef[at + 3, place, :, lanes] * minus
                        + coef[at + 4, place, :, lanes] * up[half]
                        + coef[at + 5, place, :, lanes] * down[half]
                    )
            for half, lanes in enumerate(halves):
                part[pl.ds(p, 1), :, lanes] = total[half]
            return carry

        lax.fori_loop(0, 8, one, 0, unroll=True)

    def end_step(planes, base, edge, put):
        own = plane_of(planes, base)

        def one(p, carry):
            place = pl.ds(4 + p, 1)
            for half, lanes in enumerate(halves):
                total = part[pl.ds(p, 1), :, lanes]
                around = edge(p, lanes)
                for k in range(1, 5):
                    at = 1 + 6 * (k - 1)
                    plus = jnp.where(row >= 8 - k, pltpu.roll(around, 8 - k, 1), 0.0)
                    minus = jnp.where(row < k, pltpu.roll(around, k, 1), 0.0)
                    total = (
                        total
                        + coef[at, place, :, lanes] * own(p, lanes, k)
                        + coef[at + 1, place, :, lanes] * own(p, lanes, -k)
                        + coef[at + 2, place, :, lanes] * plus
                        + coef[at + 3, place, :, lanes] * minus
                    )
                put(p, lanes, total, half)
            return carry

        lax.fori_loop(0, 8, one, 0, unroll=True)

    def back_step(level):
        backs[level].received()
        before = plane_of(back_old, 0) if level == 0 else plane_of(back.at[level - 1], 4)
        target = last.at[1] if level == STEPS - 1 else back.at[level + 1]
        start = 0 if level == STEPS - 1 else 4

        def put(p, lanes, value, half):
            if half == 0:
                value = value + inject[STEPS - 1 - level, pl.ds(p, 1)]
            target[pl.ds(start + p, 1), :, lanes] = value

        inner_step(back.at[level], back_y.at[level], before, put)
        if level < STEPS - 1:
            backs.append(
                Group(
                    shallow(back.at[level + 1], 4, back.at[level + 1], back_y.at[level + 1]),
                    back_send.at[level + 1],
                    back_recv.at[level + 1],
                )
            )

    def send_ahead(level):
        group = Group(
            shallow(ahead.at[level], 4, ahead.at[level], ahead_y.at[level]),
            ahead_send.at[level],
            ahead_recv.at[level],
        )
        groups.append(group)
        return group

    outer_model = Group(outer_model, outer_send, outer_recv)
    groups.append(outer_model)

    own_model[2].wait()
    arrived = pieces.at[pl.ds(0, n_x - 1)]
    pltpu.make_async_copy(arrived, arrived, piece_sem).wait()
    for level in (0, 1):
        found = 0.0
        for r in range(2):
            found += jnp.dot(
                picks[r],
                pieces[:, level, r, :],
                precision=lax.Precision.HIGHEST,
                preferred_element_type=f32,
            )
        found = found.reshape(8, 8, 256)
        if level == 0:
            ahead[0, 4:12] = found
            exchange = send_ahead(0)
        else:
            old[...] = found

    for copy in own_model[:2]:
        copy.wait()
    model.received()
    for half in range(2):
        dens[half, 4:20] = jnp.log(dens[half, 4:20])
        dens_ring[half, 4:12] = jnp.log(dens_ring[half, 4:12])
    coefficients(
        coef,
        ((4, 8),),
        lambda half: speed[half, 4:12],
        [dens[half, 8:16] for half in range(2)],
        lambda half, k: dens[half, 8 + k : 16 + k],
        lambda half, k: y_plus(dens[half, 8:16], dens_ring[half, 4:12], row, k),
        lambda half, k: y_minus(dens[half, 8:16], dens_ring[half, 4:12], row, k),
    )
    eye = lax.broadcasted_iota(jnp.int32, (8, 8), 0) == lax.broadcasted_iota(jnp.int32, (8, 8), 1)
    at_receiver = lax.broadcasted_iota(jnp.int32, (8, 128), 1) == REC_Z
    for x in range(8):
        sq = speed[0, 4 + x] * speed[0, 4 + x]
        for number in range(STEPS):
            line = jnp.where(eye, traces_v[number, pl.ds(x, 1), :], 0.0)
            line = jnp.sum(line, axis=1, keepdims=True)
            inject[number, x] = jnp.where(at_receiver, line, 0.0) * sq

    for copy in owns:
        copy.wait()
    back_step(0)

    begin_step(ahead.at[0], 4, plane_of(old, 0))
    exchange.received()
    end_step(ahead.at[0], 4, plane_of(ahead_y.at[0], 0), into(ahead.at[1], 4))
    exchange = send_ahead(1)
    outer_model.received()
    for planes in (pl.ds(0, 4), pl.ds(20, 4)):
        dens[s, planes] = jnp.log(dens[s, planes])
    for planes in (pl.ds(0, 4), pl.ds(12, 4)):
        dens_ring[s, planes] = jnp.log(dens_ring[s, planes])
    dens_far[s] = jnp.log(dens_far[s])
    handed = [
        ref.at[s, pl.ds(start, count)]
        for ref, start, count in (
            (speed, 0, 4),
            (speed, 12, 4),
            (speed_y, 0, 8),
            (dens, 0, 4),
            (dens, 20, 4),
            (dens_ring, 0, 4),
            (dens_ring, 12, 4),
            (dens_far, 0, 8),
        )
    ]
    handed = Group([(0, 0, other, ref, ref) for ref in handed], hand_send, hand_recv)
    groups.append(handed)
    back_step(1)
    begin_step(ahead.at[1], 4, plane_of(ahead.at[0], 4))
    exchange.received()
    end_step(ahead.at[1], 4, plane_of(ahead_y.at[1], 0), into(wide, 8))
    exchange = Group(deep(wide, 8, wide, below, above, corner), deep_send, deep_recv)
    groups.append(exchange)

    back_step(2)
    handed.received()

    def both(ref, half, low, high):
        return jnp.concatenate([ref[half, low : low + 4], ref[half, high : high + 4]], axis=0)

    coefficients(
        coef,
        ((0, 4), (12, 4)),
        lambda half: both(speed, half, 0, 12),
        [both(dens, half, 4, 16) for half in range(2)],
        lambda half, k: both(dens, half, 4 + k, 16 + k),
        lambda half, k: y_plus(both(dens, half, 4, 16), both(dens_ring, half, 0, 12), row, k),
        lambda half, k: y_minus(both(dens, half, 4, 16), both(dens_ring, half, 0, 12), row, k),
    )
    dens_above = [
        jnp.where(row < 4, dens_ring[half, 4:12], dens_far[half]) for half in range(2)
    ]
    dens_below = [
        jnp.where(row < 4, dens_far[half], dens_ring[half, 4:12]) for half in range(2)
    ]
    coefficients(
        coef_y,
        ((0, 8),),
        lambda half: speed_y[half],
        [dens_ring[half, 4:12] for half in range(2)],
        lambda half, k: dens_ring[half, 4 + k : 12 + k],
        lambda half, k: y_plus_outer(dens[half, 8:16], dens_above[half], dens_below[half], row, k),
        lambda half, k: y_minus_outer(dens[half, 8:16], dens_above[half], dens_below[half], row, k),
    )

    outs = [pltpu.make_async_copy(back.at[3, pl.ds(4, 8)], adjoint_out.at[0, 1], out_sem.at[0])]
    outs[0].start()
    early = [
        ahead[1, 4:12, :, lanes] * back[3, 4:12, :, lanes]
        + wide[8:16, :, lanes] * back[2, 4:12, :, lanes]
        for lanes in halves
    ]

    begin_step(wide, 8, plane_of(ahead.at[1], 4))
    exchange.received()
    for lanes in halves:
        ring[0:4, :, lanes] = corner[0:4, :, lanes]
        ring[4:12, :, lanes] = jnp.where(row < 4, above[:, :, lanes], below[:, :, lanes])
        ring[12:16, :, lanes] = corner[4:8, :, lanes]
    low, mine, up = plane_of(below, 0), plane_of(wide, 8), plane_of(above, 0)
    steps(
        8,
        coef_y,
        0,
        plane_of(ring, 4),
        plane_of(ring, 4),
        lambda p, lanes, centre, k: y_plus_outer(
            mine(p, lanes), up(p, lanes), low(p, lanes), row, k
        ),
        lambda p, lanes, centre, k: y_minus_outer(
            mine(p, lanes), up(p, lanes), low(p, lanes), row, k
        ),
        plane_of(ahead_y.at[1], 0),
        into(mid_y, 0),
    )
    for start in (0, 12):
        around = plane_of(ring, start)
        steps(
            4,
            coef,
            start,
            plane_of(wide, 4 + start),
            plane_of(wide, 4 + start),
            lambda p, lanes, centre, k: y_plus(centre, around(p, lanes), row, k),
            lambda p, lanes, centre, k: y_minus(centre, around(p, lanes), row, k),
            plane_of(ahead.at[1], start),
            into(mid, start),
        )
    end_step(wide, 8, plane_of(ring, 4), into(mid, 4))
    outs.append(pltpu.make_async_copy(mid.at[pl.ds(4, 8)], forward_out.at[0, 1], out_sem.at[1]))
    outs[1].start()
    to_partner = []
    for start in (0, 4):
        edge = plane_of(mid_y, start)
        steps(
            4,
            coef,
            4 + start,
            plane_of(mid, 4 + start),
            plane_of(mid, 4 + start),
            lambda p, lanes, centre, k: y_plus(centre, edge(p, lanes), row, k),
            lambda p, lanes, centre, k: y_minus(centre, edge(p, lanes), row, k),
            plane_of(wide, 8 + start),
            into(last.at[0], start),
        )
        some = pl.ds(start, 4)
        inner = pl.ds(4 + start, 4)
        whole = [
            active
            * (
                early[half][start : start + 4]
                + mid[inner, :, lanes] * back[1, inner, :, lanes]
                + last[0, some, :, lanes] * back[0, inner, :, lanes]
            )
            for half, lanes in enumerate(halves)
        ]
        share[some] = jnp.where(s == 0, whole[1], whole[0])
        copy = pltpu.make_async_remote_copy(
            share.at[some],
            partner_share.at[some],
            image_sem.at[0, start // 4],
            image_sem.at[1, start // 4],
            device_id={"shot": other},
        )
        copy.start()
        to_partner.append(copy)
        image_out[some] = jnp.where(s == 0, whole[0], whole[1])
    outs.append(pltpu.make_async_copy(last.at[0], forward_out.at[0, 0], out_sem.at[2]))
    outs[2].start()

    back_step(3)
    outs.append(pltpu.make_async_copy(last.at[1], adjoint_out.at[0, 0], out_sem.at[3]))
    outs[3].start()

    gone = stored.at[pl.ds(0, n_x - 1)]
    pltpu.make_async_copy(gone, gone, piece_send).wait()
    for group in groups + backs:
        group.sent()

    for copy in to_partner:
        copy.wait()
    image_out[...] += partner_share[...]
    for copy in outs:
        copy.wait()


def finish(image, forward, adjoint, image_out, forward_out, adjoint_out, sem):
    copies = [
        pltpu.make_async_copy(src, dst, sem.at[at])
        for at, (src, dst) in enumerate(
            ((image, image_out), (forward, forward_out), (adjoint, adjoint_out))
        )
    ]
    for copy in copies:
        copy.start()
    for copy in copies:
        copy.wait()


def shards(n_x, n_y, velocity, density, stored, holders, adjoint, traces, aperture):
    f32 = jnp.float32
    anywhere = pl.BlockSpec(memory_space=pl.ANY)
    inside = pl.BlockSpec(memory_space=pltpu.VMEM)
    results = pl.pallas_call(
        functools.partial(kernel, n_x, n_y),
        out_shape=(
            pltpu.VMEM((8, 8, 128), f32),
            pltpu.VMEM((1, 2, 8, 8, 256), f32),
            pltpu.VMEM((1, 2, 8, 8, 256), f32),
        ),
        in_specs=[anywhere] * 7,
        out_specs=(inside,) * 3,
        scratch_shapes=[
            pltpu.VMEM((2, 16, 8, 256), f32),
            pltpu.VMEM((2, 8, 8, 256), f32),
            pltpu.VMEM((24, 8, 256), f32),
            pltpu.VMEM((8, 8, 256), f32),
            pltpu.VMEM((8, 8, 256), f32),
            pltpu.VMEM((8, 8, 256), f32),
            pltpu.VMEM((16, 8, 256), f32),
            pltpu.VMEM((16, 8, 256), f32),
            pltpu.VMEM((8, 8, 256), f32),
            pltpu.VMEM((8, 8, 256), f32),
            pltpu.VMEM((STEPS, 16, 8, 256), f32),
            pltpu.VMEM((STEPS, 8, 8, 256), f32),
            pltpu.VMEM((8, 8, 256), f32),
            pltpu.VMEM((2, 8, 8, 256), f32),
            pltpu.VMEM((8, 8, 256), f32),
            pltpu.VMEM((25, 16, 8, 256), f32),
            pltpu.VMEM((25, 8, 8, 256), f32),
            pltpu.VMEM((2, 24, 8, 128), f32),
            pltpu.VMEM((2, 16, 8, 128), f32),
            pltpu.VMEM((2, 8, 8, 128), f32),
            pltpu.VMEM((2, 16, 8, 128), f32),
            pltpu.VMEM((2, 8, 8, 128), f32),
            pltpu.VMEM((n_x, 2, 2, 256), f32),
            pltpu.VMEM((1, n_x), jnp.int32),
            pltpu.VMEM((STEPS, 8, 8), f32),
            pltpu.VMEM((2, 2), jnp.int32),
            pltpu.VMEM((STEPS, 8, 8, 128), f32),
            pltpu.VMEM((8, 8, 128), f32),
            pltpu.VMEM((8, 8, 128), f32),
            pltpu.SemaphoreType.DMA((3,)),
            pltpu.SemaphoreType.DMA((3,)),
            pltpu.SemaphoreType.DMA((2,)),
            pltpu.SemaphoreType.DMA,
            pltpu.SemaphoreType.DMA,
            pltpu.SemaphoreType.DMA((10,)),
            pltpu.SemaphoreType.DMA((10,)),
            pltpu.SemaphoreType.DMA((12,)),
            pltpu.SemaphoreType.DMA((12,)),
            pltpu.SemaphoreType.DMA((8,)),
            pltpu.SemaphoreType.DMA((8,)),
            pltpu.SemaphoreType.DMA((8,)),
            pltpu.SemaphoreType.DMA((8,)),
            pltpu.SemaphoreType.DMA((2, 4)),
            pltpu.SemaphoreType.DMA((2, 4)),
            pltpu.SemaphoreType.DMA((STEPS, 4)),
            pltpu.SemaphoreType.DMA((STEPS, 4)),
            pltpu.SemaphoreType.DMA((2, 2)),
            pltpu.SemaphoreType.DMA((4,)),
        ],
        compiler_params=pltpu.CompilerParams(
            collective_id=0, has_side_effects=True, vmem_limit_bytes=48 * 1024 * 1024
        ),
        cost_estimate=pl.CostEstimate(flops=8_000_000, bytes_accessed=800_000, transcendentals=0),
    )(*(
        pltpu.with_memory_space_constraint(given, pltpu.HBM)
        for given in (velocity, density, stored, holders, adjoint, traces, aperture)
    ))
    return pl.pallas_call(
        finish,
        out_shape=tuple(jax.ShapeDtypeStruct(one.shape, f32) for one in results),
        in_specs=[inside] * 3,
        out_specs=(anywhere,) * 3,
        scratch_shapes=[pltpu.SemaphoreType.DMA((3,))],
    )(*(pltpu.with_memory_space_constraint(one, pltpu.VMEM) for one in results))


def solution(mesh):
    return jax.shard_map(
        functools.partial(shards, mesh.shape["gx"], mesh.shape["gy"]),
        mesh=mesh,
        in_specs=(
            P("gx", "gy", "shot"),
            P("gx", "gy", "shot"),
            P("gx", None, ("shot", "gy"), None),
            P("gx", None),
            P("shot", None, "gx", "gy", None),
            P("shot", None, "gx", "gy"),
            P(),
        ),
        out_specs=(
            P("gx", "gy", "shot"),
            P("shot", None, "gx", "gy", None),
            P("shot", None, "gx", "gy", None),
        ),
        check_vma=False,
    )
```
